256 devices in a mesh: lat: 16 (over z_lo, y), lon: 16 (over z_hi, x, core).
Axes of the slice: x: 4, y: 4, z: 8 (z_hi: 2, z_lo: 4; z = z_hi * 4 + z_lo), core: 2. Of those that a mesh axis runs over, the one named last changes fastest.
Arguments:
- cube_cells: bfloat16 [12288, 80, 128], P(('lat', 'lon')), may hold values from -6 to 6
- block_source: int32 [720, 16, 4], P('lat', 'lon'), may hold values from 0 to 767, as said below
- block_weight: bfloat16 [720, 16, 4, 90, 128], P('lat', 'lon'), may hold values from -0.25 to 0.25
- lift_in: bfloat16 [80, 256], replicated, may hold values from -0.625 to 0.625
- lift_out: bfloat16 [256, 256], replicated, may hold values from -0.375 to 0.375
- spectral: bfloat16 [384, 256, 256], P('lon'), may hold values from -1.5 to 1.5
Outputs:
- grid_field: bfloat16 [720, 1440, 256], P('lat', 'lon')
The draws below stay inside these ranges and needn't reach their ends.
Inputs may be any that keep to these rules, and one draw needn't show every extreme that they name: `block_source`: for target row r in band i = r // 45 and longitude block J, every entry is a position among band i's 768 tiles lying cyclically within 24 positions below or above the positions J * 48 to (J + 1) * 48 - 1. In the first row of every band and block, the first entry is the lowest position of that range and the second the highest.
All inputs are finite; a program needn't handle non-finite values.
Results may differ from the reference program's by a relative error of at most 0.015.
Values may be sent and summed in bfloat16 or wider, within the bound.
No kernel may reach another device: no remote copies, remote signals or barrier semaphores. Data moves between devices by JAX's collectives and lax.ppermute only.
A program may use at most 192 MiB of HBM per device.

```python
import math
import jax
import jax.numpy as jnp
from jax import lax

CIN = 80
C = 256
NLAT = 720
NLON = 1440
L = 384
TILE = 128
K = 4
SRC_DEV = 48
RIM = 24
LAT_DEV = 45
LON_DEV = 90
BAND_TILES = 768
SRC_TILES = 12288
N_LAT = 16
N_LON = 16


def draw_block_source(key, part):
    key = jax.random.fold_in(key, 7)
    window_size = SRC_DEV + 2 * RIM
    position = jax.random.randint(key, (NLAT, N_LON, K), 0, window_size, dtype=jnp.int32)
    row_index = jnp.arange(NLAT, dtype=jnp.int32)[:, None, None]
    slot_index = jnp.arange(K, dtype=jnp.int32)[None, None, :]
    leading = row_index % LAT_DEV == 0
    position = jnp.where(leading & (slot_index == 0), 0, position)
    position = jnp.where(leading & (slot_index == 1), window_size - 1, position)
    lon_block = jnp.arange(N_LON, dtype=jnp.int32)[None, :, None]
    return ((lon_block * SRC_DEV - RIM + position) % BAND_TILES).astype(jnp.int32)


def shard_levels(rng, shape, split, smallest, high):
    loudness, own = 1.0, jax.random.fold_in(rng, 6)
    for dim, parts in split:
        steps = jnp.exp(jax.random.uniform(jax.random.fold_in(own, dim), (parts,), jnp.float32, smallest / len(split), high / len(split)))
        loudness = loudness * jnp.repeat(steps, shape[dim] // parts).reshape([-1 if axis == dim else 1 for axis in range(len(shape))])
    return loudness


def noise(rng, extent, spread, most, cuts=(), kind=jnp.bfloat16):
    loudness = shard_levels(rng, extent, cuts, -0.22, 0.18) if cuts else 1.0
    entries = jax.random.normal(rng, extent, jnp.float32) * spread * loudness
    return jnp.minimum(jnp.maximum(entries, -most), most).astype(kind)


def setup_inputs(seed: int = 0) -> dict:
    seeds = jax.random.split(jax.random.key(seed), 7)
    cube_cells = noise(seeds[0], (SRC_TILES, CIN, TILE), 1.0, 6.0, ((0, 256),))
    block_source = draw_block_source(jax.random.fold_in(seeds[6], 71), 0)
    block_weight = noise(seeds[2], (NLAT, N_LON, K, LON_DEV, TILE), (K * TILE) ** -0.5, 0.25, ((0, 16), (1, 16)))
    lift_in = noise(seeds[3], (CIN, C), CIN ** -0.5, 0.625)
    lift_out = noise(seeds[4], (C, C), C ** -0.5, 0.375)
    spectral = noise(seeds[5], (L, C, C), (C // 16) ** -0.5, 1.5, ((0, 16),))
    return dict(cube_cells=cube_cells, block_source=block_source, block_weight=block_weight, lift_in=lift_in, lift_out=lift_out, spectral=spectral)


def legendre_setup(wave_orders):
    colatitude = (jnp.arange(NLAT, dtype=jnp.float32) + 0.5) * (math.pi / NLAT)
    cosine = jnp.cos(colatitude)[None, :]
    order_col = wave_orders.astype(jnp.float32)[:, None]
    log_scale = 0.5 * (jnp.log(2.0 * order_col + 1.0) - math.log(4.0 * math.pi) + lax.lgamma(2.0 * order_col + 1.0) - 2.0 * lax.lgamma(order_col + 1.0) - order_col * math.log(4.0)) + order_col * jnp.log(jnp.sin(colatitude))[None, :]
    initial = jnp.exp(jnp.minimum(log_scale + 80.0, 0.0))
    restore = jnp.exp(jnp.maximum(log_scale, -80.0))
    quadrature = jnp.sin(colatitude) * (math.pi / NLAT) * (2.0 * math.pi / NLON)
    return (cosine, order_col, initial, restore, quadrature)

def legendre_step(degree, current, earlier, cosine, order_col, initial):
    square = degree * degree
    rising = jnp.sqrt(jnp.maximum(4.0 * square - 1.0, 1.0) / jnp.maximum(square - order_col * order_col, 1.0))
    shifted = (degree - 1.0) * (degree - 1.0)
    falling = jnp.sqrt(jnp.maximum(shifted - order_col * order_col, 0.0) / jnp.maximum(4.0 * shifted - 1.0, 1.0))
    advanced = rising * (cosine * current - falling * earlier)
    return jnp.where(degree < order_col, 0.0, jnp.where(degree == order_col, initial, advanced))

def legendre_tables(wave_orders):
    cosine, order_col, initial, restore, quadrature = legendre_setup(wave_orders)

    def advance(carry, degree_index):
        current, earlier = carry
        latest = legendre_step(degree_index.astype(jnp.float32), current, earlier, cosine, order_col, initial)
        return ((latest, current), latest * restore)
    zeroed = jnp.zeros((wave_orders.shape[0], NLAT), jnp.float32)
    _, table = lax.scan(advance, (zeroed, zeroed), jnp.arange(L, dtype=jnp.int32))
    return ((table * quadrature[None, None, :]).astype(jnp.bfloat16), table.astype(jnp.bfloat16))

def fourier_table(wave_orders):
    longitude = jnp.arange(NLON, dtype=jnp.int32)
    phase = longitude[:, None] * wave_orders[None, :] % NLON
    angle = phase.astype(jnp.float32) * (2.0 * math.pi / NLON)
    paired = jnp.stack([jnp.cos(angle), -jnp.sin(angle)], axis=2)
    return paired.reshape(NLON, 2 * wave_orders.shape[0])

def reference(cube_cells, block_source, block_weight, lift_in, lift_out, spectral):
    lat_dev = NLAT // N_LAT
    lon_dev = NLON // N_LON
    block_width = min(128, L)
    band_cells = cube_cells.reshape(N_LAT, N_LON * SRC_DEV, CIN, TILE)
    band_sources = block_source.reshape(N_LAT, lat_dev, N_LON, K)
    band_weights = block_weight.reshape(N_LAT, lat_dev, N_LON, K, lon_dev, TILE)
    all_orders = jnp.arange(L, dtype=jnp.int32)
    table_wide = fourier_table(all_orders)
    forward = table_wide.astype(jnp.bfloat16)
    factors = jnp.repeat(jnp.where(all_orders == 0, 1.0, 2.0), 2)
    inverse = (table_wide * factors[None, :]).astype(jnp.bfloat16)
    lift_first = lift_in.astype(jnp.float32)
    lift_second = lift_out.astype(jnp.float32)
    forward_wide = forward.astype(jnp.float32)
    inverse_wide = inverse.astype(jnp.float32)
    spectral_wide = spectral.astype(jnp.float32)

    def band_spectrum(inputs):
        tiles_band, source_band, weight_band = inputs
        picked = tiles_band[source_band]
        remapped = jnp.einsum('rjkts,rjkcs->rjtc', weight_band.astype(jnp.float32), picked.astype(jnp.float32)).astype(jnp.bfloat16)
        remapped = remapped.reshape(lat_dev, NLON, CIN)
        hidden = jax.nn.gelu(jnp.einsum('rtc,cd->rtd', remapped.astype(jnp.float32), lift_first)).astype(jnp.bfloat16)
        lifted = jnp.einsum('rtd,de->rte', hidden.astype(jnp.float32), lift_second).astype(jnp.bfloat16)
        return jnp.einsum('rte,tq->req', lifted.astype(jnp.float32), forward_wide).astype(jnp.bfloat16)
    spectra = lax.map(band_spectrum, (band_cells, band_sources, band_weights)).reshape(NLAT, C, L, 2)

    def group_synthesis(group_start):
        group_orders = group_start + jnp.arange(block_width, dtype=jnp.int32)
        weighted, plain = legendre_tables(group_orders)
        section = lax.dynamic_slice_in_dim(spectra, group_start, block_width, 2)
        analysis = jnp.einsum('lmt,tcmp->mcpl', weighted.astype(jnp.float32), section.astype(jnp.float32)).astype(jnp.bfloat16)
        mixed_modes = jnp.einsum('mcpl,lcd->mlpd', analysis.astype(jnp.float32), spectral_wide).astype(jnp.bfloat16)
        return jnp.einsum('lmt,mlpd->mpdt', plain.astype(jnp.float32), mixed_modes.astype(jnp.float32)).astype(jnp.bfloat16)
    synthesis = lax.map(group_synthesis, jnp.arange(0, L, block_width, dtype=jnp.int32)).reshape(2 * L, C, NLAT)

    def band_grid(band_number):
        rows_band = lax.dynamic_slice_in_dim(synthesis, band_number * lat_dev, lat_dev, 2)
        return jnp.einsum('qct,kq->tkc', rows_band.astype(jnp.float32), inverse_wide).astype(jnp.bfloat16)
    grid_field = lax.map(band_grid, jnp.arange(N_LAT, dtype=jnp.int32)).reshape(NLAT, NLON, C)
    return grid_field
```

```python
import math

import jax
import jax.numpy as jnp
from jax import lax
from jax.experimental import pallas as pl
from jax.experimental.pallas import tpu as pltpu
from jax.sharding import PartitionSpec as P

NLAT = 720
NLON = 1440
L = 384
CIN = 80
C = 256
TILE = 128
K = 4
SRC_DEV = 48
RIM = 24
LAT_DEV = 45
LON_DEV = 90
N_LAT = 16
N_LON = 16
N_DEV = N_LAT * N_LON

ROWS = 3
GROUPS = LAT_DEV // ROWS
LON_PAD = 96
LON_ALL = N_LON * LON_PAD
ITEMS = 3
PIECES = 18
SLOTS = 24
DEG = L // N_LON
LATS = ROWS * N_DEV
MIB = 1024 * 1024


def params(mib):
    return pltpu.CompilerParams(vmem_limit_bytes=mib * MIB)


def whole():
    return pl.BlockSpec(memory_space=pltpu.VMEM)


def dot(a, b, dims=((1,), (0,))):
    return lax.dot_general(a, b, (dims, ((), ())), preferred_element_type=jnp.float32)


def remap_kernel(offsets, left, own, right, weight, out, tiles):
    step = pl.program_id(0)

    @pl.when(step == 0)
    def _():
        tiles[0:RIM] = left[...]
        tiles[RIM : RIM + SRC_DEV] = own[...]
        tiles[RIM + SRC_DEV :] = right[...]

    @pl.when(step < GROUPS)
    def _():
        columns = []
        for row in range(ROWS):
            base = (step * ROWS + row) * K
            cells = jnp.concatenate([tiles[offsets[base + k]] for k in range(K)], axis=1)
            blocks = jnp.concatenate([weight[row, 0, k] for k in range(K)], axis=1)
            columns.append(dot(blocks, cells, ((1,), (1,))))
        columns.append(jnp.zeros((LON_DEV, C - ROWS * CIN), jnp.float32))
        packed = jnp.concatenate(columns, axis=1)
        packed = jnp.concatenate([packed, jnp.zeros((LON_PAD - LON_DEV, C), jnp.float32)], axis=0)
        out[0] = packed.astype(jnp.bfloat16)

    @pl.when(step >= GROUPS)
    def _():
        out[...] = jnp.zeros_like(out)


def remap(offsets, left, own, right, weight):
    return pl.pallas_call(
        remap_kernel,
        out_shape=jax.ShapeDtypeStruct((N_LON, LON_PAD, C), jnp.bfloat16),
        grid_spec=pltpu.PrefetchScalarGridSpec(
            num_scalar_prefetch=1,
            grid=(N_LON,),
            in_specs=[
                pl.BlockSpec((RIM, CIN, TILE), lambda g, o: (0, 0, 0)),
                pl.BlockSpec((SRC_DEV, CIN, TILE), lambda g, o: (0, 0, 0)),
                pl.BlockSpec((RIM, CIN, TILE), lambda g, o: (0, 0, 0)),
                pl.BlockSpec(
                    (ROWS, 1, K, LON_DEV, TILE),
                    lambda g, o: (jnp.minimum(g, GROUPS - 1), 0, 0, 0, 0),
                ),
            ],
            out_specs=pl.BlockSpec((1, LON_PAD, C), lambda g, o: (g, 0, 0)),
            scratch_shapes=[pltpu.VMEM((RIM + SRC_DEV + RIM, CIN, TILE), jnp.bfloat16)],
        ),
        compiler_params=params(40),
        name="remap",
    )(offsets, left, own, right, weight)


def lift_kernel(cols, lift_in, lift_out, forward, out, scratch):
    for row in range(ROWS):
        hidden = jax.nn.gelu(dot(cols[...], lift_in[row])).astype(jnp.bfloat16)
        lifted = dot(hidden, lift_out[...]).astype(jnp.bfloat16)
        spectra = dot(forward[...], lifted)
        for item in range(ITEMS):
            for half in range(2):
                place = (item * ROWS + row) * 2 + half
                scratch[pl.ds(place, N_DEV, stride=SLOTS), :] = spectra[
                    item * N_DEV : (item + 1) * N_DEV, half * 128 : (half + 1) * 128
                ]
    for place in range(PIECES, SLOTS):
        scratch[pl.ds(place, N_DEV, stride=SLOTS), :] = jnp.zeros((N_DEV, 128), jnp.float32)
    out[...] = scratch[...].reshape(N_DEV, SLOTS, 128).astype(jnp.bfloat16)


def lift(cols, lift_in, lift_out, forward):
    return pl.pallas_call(
        lift_kernel,
        out_shape=jax.ShapeDtypeStruct((N_DEV, SLOTS, 128), jnp.bfloat16),
        in_specs=[whole()] * 4,
        out_specs=whole(),
        scratch_shapes=[pltpu.VMEM((N_DEV * SLOTS, 128), jnp.float32)],
        compiler_params=params(48),
        name="lift",
    )(cols, lift_in, lift_out, forward)


def legendre_kernel(rise, fall, start, initial, restore, factor, cosine, quad, weighted, plain, table):
    tiles = LATS // 128
    cos = [cosine[:, t * 128 : (t + 1) * 128] for t in range(tiles)]
    init = [initial[:, t * 128 : (t + 1) * 128] for t in range(tiles)]

    def advance(block, carry):
        current, earlier = carry
        for step in range(8):
            degree = block * 8 + step
            up, down, on = rise[degree], fall[degree], start[degree]
            latest = []
            for t in range(tiles):
                value = up * (cos[t] * current[t] - down * earlier[t]) + on * init[t]
                table[t, pl.ds(pl.multiple_of(degree * 8, 8), 8), :] = value
                latest.append(value)
            current, earlier = tuple(latest), current
        return current, earlier

    zero = tuple(jnp.zeros((8, 128), jnp.float32) for _ in range(tiles))
    lax.fori_loop(0, L // 8, advance, (zero, zero))
    for item in range(ITEMS):
        for t in range(tiles):
            lanes = slice(t * 128, (t + 1) * 128)
            values = table[t, pl.ds(item, L, stride=8), :] * restore[item : item + 1, lanes]
            weighted[item, :, lanes] = (values * quad[0:1, lanes]).astype(jnp.bfloat16)
            values = values * factor[item : item + 1, lanes]
            plain[item, lanes, :] = values.T.astype(jnp.bfloat16)


def legendre(chip):
    lane = jnp.arange(LATS, dtype=jnp.int32)
    row, device = lane // N_DEV, lane % N_DEV
    band, group = device // N_LON, device % N_LON
    held = (group < GROUPS)[None, :]
    latitude = band * LAT_DEV + jnp.minimum(group, GROUPS - 1) * ROWS + row
    colatitude = (latitude.astype(jnp.float32) + 0.5) * (math.pi / NLAT)
    cosine = jnp.cos(colatitude)[None, :]
    sine = jnp.sin(colatitude)[None, :]
    slot = jnp.arange(8, dtype=jnp.int32)
    order = (jnp.minimum(slot, ITEMS - 1) * (L // ITEMS) + chip).astype(jnp.float32)
    order_col = order[:, None]
    log_scale = (
        0.5
        * (
            jnp.log(2.0 * order_col + 1.0)
            - math.log(4.0 * math.pi)
            + lax.lgamma(2.0 * order_col + 1.0)
            - 2.0 * lax.lgamma(order_col + 1.0)
            - order_col * math.log(4.0)
        )
        + order_col * jnp.log(sine)
    )
    initial = jnp.exp(jnp.minimum(log_scale + 80.0, 0.0))
    restore = jnp.where(held, jnp.exp(jnp.maximum(log_scale, -80.0)), 0.0)
    quad = jnp.broadcast_to(sine * (math.pi / NLAT) * (2.0 * math.pi / NLON), (8, LATS))
    factor = jnp.broadcast_to(jnp.where(order_col == 0.0, 1.0, 2.0), (8, LATS))
    degree = jnp.arange(L, dtype=jnp.int32).astype(jnp.float32)[:, None, None]
    order_row = order[None, :, None]
    square = degree * degree
    rising = jnp.sqrt(
        jnp.maximum(4.0 * square - 1.0, 1.0) / jnp.maximum(square - order_row * order_row, 1.0)
    )
    shifted = (degree - 1.0) * (degree - 1.0)
    falling = jnp.sqrt(
        jnp.maximum(shifted - order_row * order_row, 0.0) / jnp.maximum(4.0 * shifted - 1.0, 1.0)
    )
    start = jnp.where(degree == order_row, 1.0, 0.0)
    spread = lambda values: jnp.broadcast_to(values, (L, 8, 128))
    return pl.pallas_call(
        legendre_kernel,
        out_shape=(
            jax.ShapeDtypeStruct((ITEMS, L, LATS), jnp.bfloat16),
            jax.ShapeDtypeStruct((ITEMS, LATS, L), jnp.bfloat16),
        ),
        in_specs=[whole()] * 8,
        out_specs=(whole(), whole()),
        scratch_shapes=[pltpu.VMEM((LATS // 128, L * 8, 128), jnp.float32)],
        compiler_params=params(40),
        name="legendre",
    )(
        spread(rising),
        spread(falling),
        spread(start),
        initial,
        restore,
        factor,
        jnp.broadcast_to(cosine, (8, LATS)),
        quad,
    )


def analyse_kernel(pieces, weighted, out, scratch):
    scratch[...] = pieces[...].astype(jnp.float32).reshape(N_DEV * SLOTS, 128)
    for item in range(ITEMS):
        rows = []
        for row in range(ROWS):
            place = (item * ROWS + row) * 2
            halves = [scratch[pl.ds(place + h, N_DEV, stride=SLOTS), :] for h in range(2)]
            rows.append(jnp.concatenate(halves, axis=1).astype(jnp.bfloat16))
        spectra = jnp.concatenate(rows, axis=0)
        result = dot(weighted[item], spectra).reshape(N_LON, DEG, C)
        out[:, item * DEG : (item + 1) * DEG, :] = result.astype(jnp.bfloat16)


def analyse(pieces, weighted):
    return pl.pallas_call(
        analyse_kernel,
        out_shape=jax.ShapeDtypeStruct((N_LON, ITEMS * DEG, C), jnp.bfloat16),
        in_specs=[whole()] * 2,
        out_specs=whole(),
        scratch_shapes=[pltpu.VMEM((N_DEV * SLOTS, 128), jnp.float32)],
        compiler_params=params(40),
        name="analyse",
    )(pieces, weighted)


MIX_STEPS = 4
MIX_DEG = DEG // MIX_STEPS


def mix_kernel(pieces, spectral, out, source, result):
    step = pl.program_id(0)
    count = N_LON * ITEMS

    @pl.when(step == 0)
    def _():
        values = pieces[...].astype(jnp.float32).reshape(count * DEG, C)
        source[0] = values[:, :128]
        source[1] = values[:, 128:]

    for index in range(MIX_DEG):
        degree = step * MIX_DEG + index
        halves = [source[h, pl.ds(degree, count, stride=DEG), :] for h in range(2)]
        values = jnp.concatenate(halves, axis=1).astype(jnp.bfloat16)
        mixed = dot(values, spectral[index])
        for h in range(2):
            result[h, pl.ds(degree, count, stride=DEG), :] = mixed[:, h * 128 : (h + 1) * 128]

    @pl.when(step == MIX_STEPS - 1)
    def _():
        for h in range(2):
            values = result[h].reshape(N_LON, ITEMS * DEG, 128)
            out[:, :, h * 128 : (h + 1) * 128] = values.astype(jnp.bfloat16)


def mix(pieces, spectral):
    shape = (N_LON, ITEMS * DEG, C)
    return pl.pallas_call(
        mix_kernel,
        out_shape=jax.ShapeDtypeStruct(shape, jnp.bfloat16),
        grid=(MIX_STEPS,),
        in_specs=[
            pl.BlockSpec(shape, lambda g: (0, 0, 0)),
            pl.BlockSpec((MIX_DEG, C, C), lambda g: (g, 0, 0)),
        ],
        out_specs=pl.BlockSpec(shape, lambda g: (0, 0, 0)),
        scratch_shapes=[pltpu.VMEM((2, N_LON * ITEMS * DEG, 128), jnp.float32)] * 2,
        compiler_params=params(40),
        name="mix",
    )(pieces, spectral)


def synthesise_kernel(pieces, plain, out, scratch):
    for item in range(ITEMS):
        values = pieces[...].astype(jnp.float32)[:, item * DEG : (item + 1) * DEG, :]
        mixed = values.reshape(L, C).astype(jnp.bfloat16)
        result = dot(plain[item], mixed)
        for row in range(ROWS):
            for half in range(2):
                place = (item * ROWS + row) * 2 + half
                scratch[pl.ds(place, N_DEV, stride=SLOTS), :] = result[
                    row * N_DEV : (row + 1) * N_DEV, half * 128 : (half + 1) * 128
                ]
    for place in range(PIECES, SLOTS):
        scratch[pl.ds(place, N_DEV, stride=SLOTS), :] = jnp.zeros((N_DEV, 128), jnp.float32)
    out[...] = scratch[...].reshape(N_DEV, SLOTS, 128).astype(jnp.bfloat16)


def synthesise(pieces, plain):
    return pl.pallas_call(
        synthesise_kernel,
        out_shape=jax.ShapeDtypeStruct((N_DEV, SLOTS, 128), jnp.bfloat16),
        in_specs=[whole()] * 2,
        out_specs=whole(),
        scratch_shapes=[pltpu.VMEM((N_DEV * SLOTS, 128), jnp.float32)],
        compiler_params=params(40),
        name="synthesise",
    )(pieces, plain)


def inverse_kernel(pieces, inverse, out, scratch):
    scratch[...] = pieces[...].astype(jnp.float32).reshape(N_DEV * SLOTS, 128)
    for row in range(ROWS):
        items = []
        for item in range(ITEMS):
            place = (item * ROWS + row) * 2
            halves = [scratch[pl.ds(place + h, N_DEV, stride=SLOTS), :] for h in range(2)]
            items.append(jnp.concatenate(halves, axis=1).astype(jnp.bfloat16))
        spectra = jnp.concatenate(items, axis=0)
        field = dot(inverse[...], spectra).astype(jnp.bfloat16)
        out[:, row * C : (row + 1) * C] = field


def invert(pieces, inverse):
    return pl.pallas_call(
        inverse_kernel,
        out_shape=jax.ShapeDtypeStruct((LON_ALL, ROWS * C), jnp.bfloat16),
        in_specs=[whole()] * 2,
        out_specs=whole(),
        scratch_shapes=[pltpu.VMEM((N_DEV * SLOTS, 128), jnp.float32)],
        compiler_params=params(48),
        name="invert",
    )(pieces, inverse)


def unpack_kernel(pieces, out):
    for row in range(ROWS):
        out[row] = pieces[0, :LON_DEV, row * C : (row + 1) * C]


def unpack(pieces):
    return pl.pallas_call(
        unpack_kernel,
        out_shape=jax.ShapeDtypeStruct((LAT_DEV, LON_DEV, C), jnp.bfloat16),
        grid=(GROUPS,),
        in_specs=[pl.BlockSpec((1, LON_PAD, ROWS * C), lambda g: (g, 0, 0))],
        out_specs=pl.BlockSpec((ROWS, LON_DEV, C), lambda g: (g, 0, 0)),
        compiler_params=params(32),
        name="unpack",
    )(pieces)


def fourier(item_axis):
    shape = (ITEMS * N_DEV, 1) if item_axis == 0 else (1, ITEMS * N_DEV)
    index = lax.broadcasted_iota(jnp.int32, shape, item_axis)
    device = index % N_DEV
    order = (index // N_DEV) * (L // ITEMS) + device // 2
    part = device % 2
    lon = lax.broadcasted_iota(
        jnp.int32, (1, LON_ALL) if item_axis == 0 else (LON_ALL, 1), 1 - item_axis
    )
    column = lon % LON_PAD
    longitude = (lon // LON_PAD) * LON_DEV + column
    held = jnp.where(column < LON_DEV, 1.0, 0.0)
    phase = longitude.astype(jnp.float32) * order.astype(jnp.float32) + 360.0 * part.astype(
        jnp.float32
    )
    phase = phase - 1440.0 * jnp.round(phase * (1.0 / 1440.0))
    angle = (360.0 - jnp.abs(phase)) * (math.pi / 720.0)
    square = angle * angle
    total = -1.0 / 39916800.0
    for term in (1.0 / 362880.0, -1.0 / 5040.0, 1.0 / 120.0, -1.0 / 6.0, 1.0):
        total = total * square + term
    return (total * angle * held).astype(jnp.bfloat16)


def exchange(values, axes):
    return lax.all_to_all(values, axes, split_axis=0, concat_axis=0, tiled=True)


def shards(cube_cells, block_source, block_weight, lift_in, lift_out, spectral):
    lat_index = lax.axis_index("lat")
    lon_index = lax.axis_index("lon")
    chip = lat_index * (N_LON // 2) + lon_index // 2
    right_pairs = [(i, (i + 1) % N_LON) for i in range(N_LON)]
    left_pairs = [(j, i) for i, j in right_pairs]
    left = lax.ppermute(cube_cells[SRC_DEV - RIM :], "lon", right_pairs)
    right = lax.ppermute(cube_cells[:RIM], "lon", left_pairs)
    offsets = (block_source[:, 0, :] - lon_index * SRC_DEV + RIM) % (N_LON * SRC_DEV)
    forward = fourier(0)
    inverse = fourier(1)
    weighted, plain = legendre(chip)
    lift_blocks = jnp.stack(
        [
            jnp.pad(lift_in, ((row * CIN, C - (row + 1) * CIN), (0, 0)))
            for row in range(ROWS)
        ]
    )
    columns = remap(offsets.reshape(LAT_DEV * K), left, cube_cells, right, block_weight)
    columns = exchange(columns, "lon").reshape(LON_ALL, C)
    spectra = exchange(lift(columns, lift_blocks, lift_out, forward), ("lat", "lon"))
    analysis = exchange(analyse(spectra, weighted), "lon")
    mixed = exchange(mix(analysis, spectral), "lon")
    synthesis = exchange(synthesise(mixed, plain), ("lat", "lon"))
    field = invert(synthesis, inverse).reshape(N_LON, LON_PAD, ROWS * C)
    return unpack(exchange(field, "lon"))


def solution(mesh):
    in_specs = (
        P(("lat", "lon"), None, None),
        P("lat", "lon", None),
        P("lat", "lon", None, None, None),
        P(),
        P(),
        P("lon", None, None),
    )
    out_specs = P("lat", "lon", None)
    return jax.shard_map(shards, mesh=mesh, in_specs=in_specs, out_specs=out_specs, check_vma=False)
```

```python
import math

import jax
import jax.numpy as jnp
from jax import lax
from jax.experimental import pallas as pl
from jax.experimental.pallas import tpu as pltpu
from jax.sharding import PartitionSpec as P

NLAT = 720
NLON = 1440
L = 384
CIN = 80
C = 256
TILE = 128
K = 4
SRC_DEV = 48
RIM = 24
LAT_DEV = 45
LON_DEV = 90
N_LAT = 16
N_LON = 16
N_DEV = N_LAT * N_LON

ROWS = 3
GROUPS = LAT_DEV // ROWS
ITEMS = 3
PIECES = 2 * ITEMS * ROWS
DEG = L // N_LON
LATS = ROWS * N_DEV
MIB = 1024 * 1024


def params(mib):
    return pltpu.CompilerParams(vmem_limit_bytes=mib * MIB)


def whole():
    return pl.BlockSpec(memory_space=pltpu.VMEM)


def dot(a, b, dims=((1,), (0,))):
    return lax.dot_general(a, b, (dims, ((), ())), preferred_element_type=jnp.float32)


REMAP_STEPS = 4
STEP_GROUPS = N_LON // REMAP_STEPS
GROUP_ROWS = 2 * LON_DEV


def remap_kernel(offsets, left, own, right, weight, out, tiles, packed):
    step = pl.program_id(0)

    @pl.when(step == 0)
    def _():
        tiles[0:RIM] = left[...]
        tiles[RIM : RIM + SRC_DEV] = own[...]
        tiles[RIM + SRC_DEV :] = right[...]

    def store(sub, values):
        for half in range(2):
            packed[pl.ds(sub * GROUP_ROWS + half, LON_DEV, stride=2), :] = values[
                :, half * 128 : (half + 1) * 128
            ]

    def fill(sub):
        columns = []
        for row in range(ROWS):
            base = ((step * STEP_GROUPS + sub) * ROWS + row) * K
            cells = jnp.concatenate([tiles[offsets[base + k]] for k in range(K)], axis=1)
            blocks = jnp.concatenate([weight[sub * ROWS + row, 0, k] for k in range(K)], axis=1)
            columns.append(dot(blocks, cells, ((1,), (1,))))
        columns.append(jnp.zeros((LON_DEV, C - ROWS * CIN), jnp.float32))
        store(sub, jnp.concatenate(columns, axis=1))

    for sub in range(STEP_GROUPS - 1):
        fill(sub)

    @pl.when(step < REMAP_STEPS - 1)
    def _():
        fill(STEP_GROUPS - 1)

    @pl.when(step == REMAP_STEPS - 1)
    def _():
        store(STEP_GROUPS - 1, jnp.zeros((LON_DEV, C), jnp.float32))

    out[...] = packed[...].astype(jnp.bfloat16)


def remap(offsets, left, own, right, weight):
    return pl.pallas_call(
        remap_kernel,
        out_shape=jax.ShapeDtypeStruct((N_LON * GROUP_ROWS, 128), jnp.bfloat16),
        grid_spec=pltpu.PrefetchScalarGridSpec(
            num_scalar_prefetch=1,
            grid=(REMAP_STEPS,),
            in_specs=[
                pl.BlockSpec((RIM, CIN, TILE), lambda g, o: (0, 0, 0)),
                pl.BlockSpec((SRC_DEV, CIN, TILE), lambda g, o: (0, 0, 0)),
                pl.BlockSpec((RIM, CIN, TILE), lambda g, o: (0, 0, 0)),
                pl.BlockSpec(
                    (STEP_GROUPS * ROWS, 1, K, LON_DEV, TILE), lambda g, o: (g, 0, 0, 0, 0)
                ),
            ],
            out_specs=pl.BlockSpec((STEP_GROUPS * GROUP_ROWS, 128), lambda g, o: (g, 0)),
            scratch_shapes=[
                pltpu.VMEM((RIM + SRC_DEV + RIM, CIN, TILE), jnp.bfloat16),
                pltpu.VMEM((STEP_GROUPS * GROUP_ROWS, 128), jnp.float32),
            ],
        ),
        compiler_params=params(40),
        name="remap",
    )(offsets, left, own, right, weight)


def lift_kernel(cols, lift_in, lift_out, forward, out, packed, scratch):
    packed[...] = cols[...].astype(jnp.float32)
    halves = [packed[pl.ds(h, NLON, stride=2), :] for h in range(2)]
    values = jnp.concatenate(halves, axis=1).astype(jnp.bfloat16)
    for row in range(ROWS):
        hidden = jax.nn.gelu(dot(values, lift_in[row])).astype(jnp.bfloat16)
        lifted = dot(hidden, lift_out[...]).astype(jnp.bfloat16)
        spectra = dot(forward[...], lifted)
        for item in range(ITEMS):
            for half in range(2):
                place = (item * ROWS + row) * 2 + half
                scratch[pl.ds(place, N_DEV, stride=PIECES), :] = spectra[
                    item * N_DEV : (item + 1) * N_DEV, half * 128 : (half + 1) * 128
                ]
    out[...] = scratch[...].astype(jnp.bfloat16)


def lift(cols, lift_in, lift_out, forward):
    return pl.pallas_call(
        lift_kernel,
        out_shape=jax.ShapeDtypeStruct((N_DEV * PIECES, 128), jnp.bfloat16),
        in_specs=[whole()] * 4,
        out_specs=whole(),
        scratch_shapes=[
            pltpu.VMEM((2 * NLON, 128), jnp.float32),
            pltpu.VMEM((N_DEV * PIECES, 128), jnp.float32),
        ],
        compiler_params=params(48),
        name="lift",
    )(cols, lift_in, lift_out, forward)


def legendre_kernel(rise, fall, start, initial, restore, factor, cosine, quad, weighted, plain, table):
    tiles = LATS // 128
    cos = [cosine[:, t * 128 : (t + 1) * 128] for t in range(tiles)]
    init = [initial[:, t * 128 : (t + 1) * 128] for t in range(tiles)]

    def advance(block, carry):
        current, earlier = carry
        for step in range(8):
            degree = block * 8 + step
            up, down, on = rise[degree], fall[degree], start[degree]
            latest = []
            for t in range(tiles):
                value = up * (cos[t] * current[t] - down * earlier[t]) + on * init[t]
                table[t, pl.ds(pl.multiple_of(degree * 8, 8), 8), :] = value
                latest.append(value)
            current, earlier = tuple(latest), current
        return current, earlier

    zero = tuple(jnp.zeros((8, 128), jnp.float32) for _ in range(tiles))
    lax.fori_loop(0, L // 8, advance, (zero, zero))
    for item in range(ITEMS):
        for t in range(tiles):
            lanes = slice(t * 128, (t + 1) * 128)
            values = table[t, pl.ds(item, L, stride=8), :] * restore[item : item + 1, lanes]
            weighted[item, :, lanes] = (values * quad[0:1, lanes]).astype(jnp.bfloat16)
            values = values * factor[item : item + 1, lanes]
            plain[item, lanes, :] = values.T.astype(jnp.bfloat16)


def legendre(chip):
    lane = jnp.arange(LATS, dtype=jnp.int32)
    row, device = lane // N_DEV, lane % N_DEV
    band, group = device // N_LON, device % N_LON
    held = (group < GROUPS)[None, :]
    latitude = band * LAT_DEV + jnp.minimum(group, GROUPS - 1) * ROWS + row
    colatitude = (latitude.astype(jnp.float32) + 0.5) * (math.pi / NLAT)
    cosine = jnp.cos(colatitude)[None, :]
    sine = jnp.sin(colatitude)[None, :]
    slot = jnp.arange(8, dtype=jnp.int32)
    order = (jnp.minimum(slot, ITEMS - 1) * (L // ITEMS) + chip).astype(jnp.float32)
    order_col = order[:, None]
    log_scale = (
        0.5
        * (
            jnp.log(2.0 * order_col + 1.0)
            - math.log(4.0 * math.pi)
            + lax.lgamma(2.0 * order_col + 1.0)
            - 2.0 * lax.lgamma(order_col + 1.0)
            - order_col * math.log(4.0)
        )
        + order_col * jnp.log(sine)
    )
    initial = jnp.exp(jnp.minimum(log_scale + 80.0, 0.0))
    restore = jnp.where(held, jnp.exp(jnp.maximum(log_scale, -80.0)), 0.0)
    quad = jnp.broadcast_to(sine * (math.pi / NLAT) * (2.0 * math.pi / NLON), (8, LATS))
    factor = jnp.broadcast_to(jnp.where(order_col == 0.0, 1.0, 2.0), (8, LATS))
    degree = jnp.arange(L, dtype=jnp.int32).astype(jnp.float32)[:, None, None]
    order_row = order[None, :, None]
    square = degree * degree
    rising = jnp.sqrt(
        jnp.maximum(4.0 * square - 1.0, 1.0) / jnp.maximum(square - order_row * order_row, 1.0)
    )
    shifted = (degree - 1.0) * (degree - 1.0)
    falling = jnp.sqrt(
        jnp.maximum(shifted - order_row * order_row, 0.0) / jnp.maximum(4.0 * shifted - 1.0, 1.0)
    )
    start = jnp.where(degree == order_row, 1.0, 0.0)
    spread = lambda values: jnp.broadcast_to(values, (L, 8, 128))
    return pl.pallas_call(
        legendre_kernel,
        out_shape=(
            jax.ShapeDtypeStruct((ITEMS, L, LATS), jnp.bfloat16),
            jax.ShapeDtypeStruct((ITEMS, LATS, L), jnp.bfloat16),
        ),
        in_specs=[whole()] * 8,
        out_specs=(whole(), whole()),
        scratch_shapes=[pltpu.VMEM((LATS // 128, L * 8, 128), jnp.float32)],
        compiler_params=params(40),
        name="legendre",
    )(
        spread(rising),
        spread(falling),
        spread(start),
        initial,
        restore,
        factor,
        jnp.broadcast_to(cosine, (8, LATS)),
        quad,
    )


def analyse_kernel(pieces, weighted, out, scratch):
    scratch[...] = pieces[...].astype(jnp.float32)
    for item in range(ITEMS):
        rows = []
        for row in range(ROWS):
            place = (item * ROWS + row) * 2
            halves = [scratch[pl.ds(place + h, N_DEV, stride=PIECES), :] for h in range(2)]
            rows.append(jnp.concatenate(halves, axis=1).astype(jnp.bfloat16))
        spectra = jnp.concatenate(rows, axis=0)
        result = dot(weighted[item], spectra).reshape(N_LON, DEG, C)
        out[:, item * DEG : (item + 1) * DEG, :] = result.astype(jnp.bfloat16)


def analyse(pieces, weighted):
    return pl.pallas_call(
        analyse_kernel,
        out_shape=jax.ShapeDtypeStruct((N_LON, ITEMS * DEG, C), jnp.bfloat16),
        in_specs=[whole()] * 2,
        out_specs=whole(),
        scratch_shapes=[pltpu.VMEM((N_DEV * PIECES, 128), jnp.float32)],
        compiler_params=params(40),
        name="analyse",
    )(pieces, weighted)


MIX_STEPS = 4
MIX_DEG = DEG // MIX_STEPS


def mix_kernel(pieces, spectral, out, source, result):
    step = pl.program_id(0)
    count = N_LON * ITEMS

    @pl.when(step == 0)
    def _():
        values = pieces[...].astype(jnp.float32).reshape(count * DEG, C)
        source[0] = values[:, :128]
        source[1] = values[:, 128:]

    for index in range(MIX_DEG):
        degree = step * MIX_DEG + index
        halves = [source[h, pl.ds(degree, count, stride=DEG), :] for h in range(2)]
        values = jnp.concatenate(halves, axis=1).astype(jnp.bfloat16)
        mixed = dot(values, spectral[index])
        for h in range(2):
            result[h, pl.ds(degree, count, stride=DEG), :] = mixed[:, h * 128 : (h + 1) * 128]

    @pl.when(step == MIX_STEPS - 1)
    def _():
        for h in range(2):
            values = result[h].reshape(N_LON, ITEMS * DEG, 128)
            out[:, :, h * 128 : (h + 1) * 128] = values.astype(jnp.bfloat16)


def mix(pieces, spectral):
    shape = (N_LON, ITEMS * DEG, C)
    return pl.pallas_call(
        mix_kernel,
        out_shape=jax.ShapeDtypeStruct(shape, jnp.bfloat16),
        grid=(MIX_STEPS,),
        in_specs=[
            pl.BlockSpec(shape, lambda g: (0, 0, 0)),
            pl.BlockSpec((MIX_DEG, C, C), lambda g: (g, 0, 0)),
        ],
        out_specs=pl.BlockSpec(shape, lambda g: (0, 0, 0)),
        scratch_shapes=[pltpu.VMEM((2, N_LON * ITEMS * DEG, 128), jnp.float32)] * 2,
        compiler_params=params(40),
        name="mix",
    )(pieces, spectral)


def synthesise_kernel(pieces, plain, out, scratch):
    for item in range(ITEMS):
        values = pieces[...].astype(jnp.float32)[:, item * DEG : (item + 1) * DEG, :]
        mixed = values.reshape(L, C).astype(jnp.bfloat16)
        result = dot(plain[item], mixed)
        for row in range(ROWS):
            for half in range(2):
                place = (item * ROWS + row) * 2 + half
                scratch[pl.ds(place, N_DEV, stride=PIECES), :] = result[
                    row * N_DEV : (row + 1) * N_DEV, half * 128 : (half + 1) * 128
                ]
    out[...] = scratch[...].astype(jnp.bfloat16)


def synthesise(pieces, plain):
    return pl.pallas_call(
        synthesise_kernel,
        out_shape=jax.ShapeDtypeStruct((N_DEV * PIECES, 128), jnp.bfloat16),
        in_specs=[whole()] * 2,
        out_specs=whole(),
        scratch_shapes=[pltpu.VMEM((N_DEV * PIECES, 128), jnp.float32)],
        compiler_params=params(40),
        name="synthesise",
    )(pieces, plain)


TILES = 2 * ROWS


def inverse_kernel(pieces, inverse, out, scratch, packed):
    scratch[...] = pieces[...].astype(jnp.float32)
    for row in range(ROWS):
        items = []
        for item in range(ITEMS):
            place = (item * ROWS + row) * 2
            halves = [scratch[pl.ds(place + h, N_DEV, stride=PIECES), :] for h in range(2)]
            items.append(jnp.concatenate(halves, axis=1).astype(jnp.bfloat16))
        spectra = jnp.concatenate(items, axis=0)
        field = dot(inverse[...], spectra)
        for half in range(2):
            packed[pl.ds(row * 2 + half, NLON, stride=TILES), :] = field[
                :, half * 128 : (half + 1) * 128
            ]
    out[...] = packed[...].astype(jnp.bfloat16)


def invert(pieces, inverse):
    return pl.pallas_call(
        inverse_kernel,
        out_shape=jax.ShapeDtypeStruct((NLON * TILES, 128), jnp.bfloat16),
        in_specs=[whole()] * 2,
        out_specs=whole(),
        scratch_shapes=[
            pltpu.VMEM((N_DEV * PIECES, 128), jnp.float32),
            pltpu.VMEM((NLON * TILES, 128), jnp.float32),
        ],
        compiler_params=params(48),
        name="invert",
    )(pieces, inverse)


UNPACK_GROUPS = 4


def unpack_kernel(pieces, out, packed):
    packed[...] = pieces[...].astype(jnp.float32)
    for group in range(UNPACK_GROUPS):
        for row in range(ROWS):
            place = group * LON_DEV * TILES + row * 2
            halves = [packed[pl.ds(place + h, LON_DEV, stride=TILES), :] for h in range(2)]
            out[group * ROWS + row] = jnp.concatenate(halves, axis=1).astype(jnp.bfloat16)


def unpack(pieces):
    block = UNPACK_GROUPS * LON_DEV * TILES
    return pl.pallas_call(
        unpack_kernel,
        out_shape=jax.ShapeDtypeStruct((LAT_DEV, LON_DEV, C), jnp.bfloat16),
        grid=(N_LON // UNPACK_GROUPS,),
        in_specs=[pl.BlockSpec((block, 128), lambda g: (g, 0))],
        out_specs=pl.BlockSpec((UNPACK_GROUPS * ROWS, LON_DEV, C), lambda g: (g, 0, 0)),
        scratch_shapes=[pltpu.VMEM((block, 128), jnp.float32)],
        compiler_params=params(32),
        name="unpack",
    )(pieces)


def fourier(item_axis):
    shape = (ITEMS * N_DEV, 1) if item_axis == 0 else (1, ITEMS * N_DEV)
    index = lax.broadcasted_iota(jnp.int32, shape, item_axis)
    device = index % N_DEV
    order = (index // N_DEV) * (L // ITEMS) + device // 2
    part = device % 2
    longitude = lax.broadcasted_iota(
        jnp.int32, (1, NLON) if item_axis == 0 else (NLON, 1), 1 - item_axis
    )
    phase = longitude.astype(jnp.float32) * order.astype(jnp.float32) + 360.0 * part.astype(
        jnp.float32
    )
    phase = phase - 1440.0 * jnp.round(phase * (1.0 / 1440.0))
    angle = (360.0 - jnp.abs(phase)) * (math.pi / 720.0)
    square = angle * angle
    total = -1.0 / 39916800.0
    for term in (1.0 / 362880.0, -1.0 / 5040.0, 1.0 / 120.0, -1.0 / 6.0, 1.0):
        total = total * square + term
    return (total * angle).astype(jnp.bfloat16)


def exchange(values, axes, count):
    pairs = values.reshape(count, values.shape[0] // (2 * count), 2, 128)
    pairs = lax.all_to_all(pairs, axes, split_axis=0, concat_axis=0, tiled=True)
    return pairs.reshape(values.shape)


def regroup(values):
    return lax.all_to_all(values, "lon", split_axis=0, concat_axis=0, tiled=True)


def shards(cube_cells, block_source, block_weight, lift_in, lift_out, spectral):
    lat_index = lax.axis_index("lat")
    lon_index = lax.axis_index("lon")
    chip = lat_index * (N_LON // 2) + lon_index // 2
    right_pairs = [(i, (i + 1) % N_LON) for i in range(N_LON)]
    left_pairs = [(j, i) for i, j in right_pairs]
    left = lax.ppermute(cube_cells[SRC_DEV - RIM :], "lon", right_pairs)
    right = lax.ppermute(cube_cells[:RIM], "lon", left_pairs)
    offsets = (block_source[:, 0, :] - lon_index * SRC_DEV + RIM) % (N_LON * SRC_DEV)
    forward = fourier(0)
    inverse = fourier(1)
    weighted, plain = legendre(chip)
    lift_blocks = jnp.stack(
        [
            jnp.pad(lift_in, ((row * CIN, C - (row + 1) * CIN), (0, 0)))
            for row in range(ROWS)
        ]
    )
    columns = remap(offsets.reshape(LAT_DEV * K), left, cube_cells, right, block_weight)
    columns = exchange(columns, "lon", N_LON)
    spectra = lift(columns, lift_blocks, lift_out, forward)
    spectra = exchange(spectra, ("lat", "lon"), N_DEV)
    analysis = regroup(analyse(spectra, weighted))
    mixed = regroup(mix(analysis, spectral))
    synthesis = exchange(synthesise(mixed, plain), ("lat", "lon"), N_DEV)
    field = exchange(invert(synthesis, inverse), "lon", N_LON)
    return unpack(field)


def solution(mesh):
    in_specs = (
        P(("lat", "lon"), None, None),
        P("lat", "lon", None),
        P("lat", "lon", None, None, None),
        P(),
        P(),
        P("lon", None, None),
    )
    out_specs = P("lat", "lon", None)
    return jax.shard_map(shards, mesh=mesh, in_specs=in_specs, out_specs=out_specs, check_vma=False)
```

```python
import math

import jax
import jax.numpy as jnp
from jax import lax
from jax.experimental import pallas as pl
from jax.experimental.pallas import tpu as pltpu
from jax.sharding import PartitionSpec as P

NLAT = 720
NLON = 1440
L = 384
CIN = 80
C = 256
TILE = 128
K = 4
SRC_DEV = 48
RIM = 24
LAT_DEV = 45
LON_DEV = 90
N_LAT = 16
N_LON = 16
N_DEV = N_LAT * N_LON

ROWS = 3
GROUPS = LAT_DEV // ROWS
ITEMS = 3
PIECES = 2 * ITEMS * ROWS
DEG = L // N_LON
LATS = ROWS * N_DEV
MIB = 1024 * 1024


def params(mib):
    return pltpu.CompilerParams(vmem_limit_bytes=mib * MIB)


def whole():
    return pl.BlockSpec(memory_space=pltpu.VMEM)


def dot(a, b, dims=((1,), (0,))):
    return lax.dot_general(a, b, (dims, ((), ())), preferred_element_type=jnp.float32)


REMAP_STEPS = 4
STEP_GROUPS = N_LON // REMAP_STEPS
GROUP_ROWS = 2 * LON_DEV


def remap_kernel(offsets, across, own, beside, weight, out, tiles, packed):
    step = pl.program_id(0)

    @pl.when(step == 0)
    def _():
        place = offsets[LAT_DEV * K]
        tiles[pl.ds(place, RIM)] = across[...]
        tiles[pl.ds(RIM + SRC_DEV - place, RIM)] = beside[...]
        tiles[RIM : RIM + SRC_DEV] = own[...]

    def store(sub, values):
        for half in range(2):
            packed[pl.ds(sub * GROUP_ROWS + half, LON_DEV, stride=2), :] = values[
                :, half * 128 : (half + 1) * 128
            ]

    def fill(sub):
        columns = []
        for row in range(ROWS):
            base = ((step * STEP_GROUPS + sub) * ROWS + row) * K
            cells = jnp.concatenate([tiles[offsets[base + k]] for k in range(K)], axis=1)
            blocks = jnp.concatenate([weight[sub * ROWS + row, 0, k] for k in range(K)], axis=1)
            columns.append(dot(blocks, cells, ((1,), (1,))))
        columns.append(jnp.zeros((LON_DEV, C - ROWS * CIN), jnp.float32))
        store(sub, jnp.concatenate(columns, axis=1))

    for sub in range(STEP_GROUPS - 1):
        fill(sub)

    @pl.when(step < REMAP_STEPS - 1)
    def _():
        fill(STEP_GROUPS - 1)

    @pl.when(step == REMAP_STEPS - 1)
    def _():
        store(STEP_GROUPS - 1, jnp.zeros((LON_DEV, C), jnp.float32))

    out[...] = packed[...].astype(jnp.bfloat16)


def remap(offsets, across, own, beside, weight):
    return pl.pallas_call(
        remap_kernel,
        out_shape=jax.ShapeDtypeStruct((N_LON * GROUP_ROWS, 128), jnp.bfloat16),
        grid_spec=pltpu.PrefetchScalarGridSpec(
            num_scalar_prefetch=1,
            grid=(REMAP_STEPS,),
            in_specs=[
                pl.BlockSpec((RIM, CIN, TILE), lambda g, o: (0, 0, 0)),
                pl.BlockSpec((SRC_DEV, CIN, TILE), lambda g, o: (0, 0, 0)),
                pl.BlockSpec((RIM, CIN, TILE), lambda g, o: (0, 0, 0)),
                pl.BlockSpec(
                    (STEP_GROUPS * ROWS, 1, K, LON_DEV, TILE), lambda g, o: (g, 0, 0, 0, 0)
                ),
            ],
            out_specs=pl.BlockSpec((STEP_GROUPS * GROUP_ROWS, 128), lambda g, o: (g, 0)),
            scratch_shapes=[
                pltpu.VMEM((RIM + SRC_DEV + RIM, CIN, TILE), jnp.bfloat16),
                pltpu.VMEM((STEP_GROUPS * GROUP_ROWS, 128), jnp.float32),
            ],
        ),
        compiler_params=params(40),
        name="remap",
    )(offsets, across, own, beside, weight)


def lift_kernel(cols, lift_in, lift_out, forward, *rest):
    out, packed, scratch = rest[-3:]
    packed[...] = cols[...].astype(jnp.float32)
    halves = [packed[pl.ds(h, NLON, stride=2), :] for h in range(2)]
    values = jnp.concatenate(halves, axis=1).astype(jnp.bfloat16)
    for row in range(ROWS):
        hidden = jax.nn.gelu(dot(values, lift_in[row])).astype(jnp.bfloat16)
        lifted = dot(hidden, lift_out[...]).astype(jnp.bfloat16)
        spectra = dot(forward[...], lifted)
        for item in range(ITEMS):
            for half in range(2):
                place = (item * ROWS + row) * 2 + half
                scratch[pl.ds(place, N_DEV, stride=PIECES), :] = spectra[
                    item * N_DEV : (item + 1) * N_DEV, half * 128 : (half + 1) * 128
                ]
    out[...] = scratch[...].astype(jnp.bfloat16)


def lift(cols, lift_in, lift_out, forward, tables):
    return pl.pallas_call(
        lift_kernel,
        out_shape=jax.ShapeDtypeStruct((N_DEV * PIECES, 128), jnp.bfloat16),
        in_specs=[whole()] * 4 + [pl.BlockSpec(memory_space=pl.ANY)] * len(tables),
        out_specs=whole(),
        scratch_shapes=[
            pltpu.VMEM((2 * NLON, 128), jnp.float32),
            pltpu.VMEM((N_DEV * PIECES, 128), jnp.float32),
        ],
        compiler_params=params(48),
        name="lift",
    )(cols, lift_in, lift_out, forward, *tables)


def legendre_kernel(rise, fall, start, initial, restore, factor, cosine, quad, weighted, plain, table):
    tiles = LATS // 128
    cos = [cosine[:, t * 128 : (t + 1) * 128] for t in range(tiles)]
    init = [initial[:, t * 128 : (t + 1) * 128] for t in range(tiles)]

    def advance(block, carry):
        current, earlier = carry
        for step in range(8):
            degree = block * 8 + step
            up, down, on = rise[degree], fall[degree], start[degree]
            latest = []
            for t in range(tiles):
                value = up * (cos[t] * current[t] - down * earlier[t]) + on * init[t]
                table[t, pl.ds(pl.multiple_of(degree * 8, 8), 8), :] = value
                latest.append(value)
            current, earlier = tuple(latest), current
        return current, earlier

    zero = tuple(jnp.zeros((8, 128), jnp.float32) for _ in range(tiles))
    lax.fori_loop(0, L // 8, advance, (zero, zero))
    for item in range(ITEMS):
        for t in range(tiles):
            lanes = slice(t * 128, (t + 1) * 128)
            values = table[t, pl.ds(item, L, stride=8), :] * restore[item : item + 1, lanes]
            weighted[item, :, lanes] = (values * quad[0:1, lanes]).astype(jnp.bfloat16)
            values = values * factor[item : item + 1, lanes]
            plain[item, lanes, :] = values.T.astype(jnp.bfloat16)


def legendre(chip):
    lane = jnp.arange(LATS, dtype=jnp.int32)
    row, device = lane // N_DEV, lane % N_DEV
    band, group = device // N_LON, device % N_LON
    held = (group < GROUPS)[None, :]
    latitude = band * LAT_DEV + jnp.minimum(group, GROUPS - 1) * ROWS + row
    colatitude = (latitude.astype(jnp.float32) + 0.5) * (math.pi / NLAT)
    cosine = jnp.cos(colatitude)[None, :]
    sine = jnp.sin(colatitude)[None, :]
    slot = jnp.arange(8, dtype=jnp.int32)
    order = (jnp.minimum(slot, ITEMS - 1) * (L // ITEMS) + chip).astype(jnp.float32)
    order_col = order[:, None]
    log_scale = (
        0.5
        * (
            jnp.log(2.0 * order_col + 1.0)
            - math.log(4.0 * math.pi)
            + lax.lgamma(2.0 * order_col + 1.0)
            - 2.0 * lax.lgamma(order_col + 1.0)
            - order_col * math.log(4.0)
        )
        + order_col * jnp.log(sine)
    )
    initial = jnp.exp(jnp.minimum(log_scale + 80.0, 0.0))
    restore = jnp.where(held, jnp.exp(jnp.maximum(log_scale, -80.0)), 0.0)
    quad = jnp.broadcast_to(sine * (math.pi / NLAT) * (2.0 * math.pi / NLON), (8, LATS))
    factor = jnp.broadcast_to(jnp.where(order_col == 0.0, 1.0, 2.0), (8, LATS))
    degree = jnp.arange(L, dtype=jnp.int32).astype(jnp.float32)[:, None, None]
    order_row = order[None, :, None]
    square = degree * degree
    rising = jnp.sqrt(
        jnp.maximum(4.0 * square - 1.0, 1.0) / jnp.maximum(square - order_row * order_row, 1.0)
    )
    shifted = (degree - 1.0) * (degree - 1.0)
    falling = jnp.sqrt(
        jnp.maximum(shifted - order_row * order_row, 0.0) / jnp.maximum(4.0 * shifted - 1.0, 1.0)
    )
    start = jnp.where(degree == order_row, 1.0, 0.0)
    spread = lambda values: jnp.broadcast_to(values, (L, 8, 128))
    return pl.pallas_call(
        legendre_kernel,
        out_shape=(
            jax.ShapeDtypeStruct((ITEMS, L, LATS), jnp.bfloat16),
            jax.ShapeDtypeStruct((ITEMS, LATS, L), jnp.bfloat16),
        ),
        in_specs=[whole()] * 8,
        out_specs=(whole(), whole()),
        scratch_shapes=[pltpu.VMEM((LATS // 128, L * 8, 128), jnp.float32)],
        compiler_params=params(40),
        name="legendre",
    )(
        spread(rising),
        spread(falling),
        spread(start),
        initial,
        restore,
        factor,
        jnp.broadcast_to(cosine, (8, LATS)),
        quad,
    )


def analyse_kernel(pieces, weighted, out, scratch):
    scratch[...] = pieces[...].astype(jnp.float32)
    for item in range(ITEMS):
        rows = []
        for row in range(ROWS):
            place = (item * ROWS + row) * 2
            halves = [scratch[pl.ds(place + h, N_DEV, stride=PIECES), :] for h in range(2)]
            rows.append(jnp.concatenate(halves, axis=1).astype(jnp.bfloat16))
        spectra = jnp.concatenate(rows, axis=0)
        result = dot(weighted[item], spectra).reshape(N_LON, DEG, C)
        out[:, item * DEG : (item + 1) * DEG, :] = result.astype(jnp.bfloat16)


def analyse(pieces, weighted):
    return pl.pallas_call(
        analyse_kernel,
        out_shape=jax.ShapeDtypeStruct((N_LON, ITEMS * DEG, C), jnp.bfloat16),
        in_specs=[whole()] * 2,
        out_specs=whole(),
        scratch_shapes=[pltpu.VMEM((N_DEV * PIECES, 128), jnp.float32)],
        compiler_params=params(40),
        name="analyse",
    )(pieces, weighted)


MIX_STEPS = 4
MIX_DEG = DEG // MIX_STEPS


def mix_kernel(pieces, spectral, out, source, result):
    step = pl.program_id(0)
    count = N_LON * ITEMS

    @pl.when(step == 0)
    def _():
        values = pieces[...].astype(jnp.float32).reshape(count * DEG, C)
        source[0] = values[:, :128]
        source[1] = values[:, 128:]

    for index in range(MIX_DEG):
        degree = step * MIX_DEG + index
        halves = [source[h, pl.ds(degree, count, stride=DEG), :] for h in range(2)]
        values = jnp.concatenate(halves, axis=1).astype(jnp.bfloat16)
        mixed = dot(values, spectral[index])
        for h in range(2):
            result[h, pl.ds(degree, count, stride=DEG), :] = mixed[:, h * 128 : (h + 1) * 128]

    @pl.when(step == MIX_STEPS - 1)
    def _():
        for h in range(2):
            values = result[h].reshape(N_LON, ITEMS * DEG, 128)
            out[:, :, h * 128 : (h + 1) * 128] = values.astype(jnp.bfloat16)


def mix(pieces, spectral):
    shape = (N_LON, ITEMS * DEG, C)
    return pl.pallas_call(
        mix_kernel,
        out_shape=jax.ShapeDtypeStruct(shape, jnp.bfloat16),
        grid=(MIX_STEPS,),
        in_specs=[
            pl.BlockSpec(shape, lambda g: (0, 0, 0)),
            pl.BlockSpec((MIX_DEG, C, C), lambda g: (g, 0, 0)),
        ],
        out_specs=pl.BlockSpec(shape, lambda g: (0, 0, 0)),
        scratch_shapes=[pltpu.VMEM((2, N_LON * ITEMS * DEG, 128), jnp.float32)] * 2,
        compiler_params=params(40),
        name="mix",
    )(pieces, spectral)


def synthesise_kernel(pieces, plain, out, scratch):
    for item in range(ITEMS):
        values = pieces[...].astype(jnp.float32)[:, item * DEG : (item + 1) * DEG, :]
        mixed = values.reshape(L, C).astype(jnp.bfloat16)
        result = dot(plain[item], mixed)
        for row in range(ROWS):
            for half in range(2):
                place = (item * ROWS + row) * 2 + half
                scratch[pl.ds(place, N_DEV, stride=PIECES), :] = result[
                    row * N_DEV : (row + 1) * N_DEV, half * 128 : (half + 1) * 128
                ]
    out[...] = scratch[...].astype(jnp.bfloat16)


def synthesise(pieces, plain):
    return pl.pallas_call(
        synthesise_kernel,
        out_shape=jax.ShapeDtypeStruct((N_DEV * PIECES, 128), jnp.bfloat16),
        in_specs=[whole()] * 2,
        out_specs=whole(),
        scratch_shapes=[pltpu.VMEM((N_DEV * PIECES, 128), jnp.float32)],
        compiler_params=params(40),
        name="synthesise",
    )(pieces, plain)


TILES = 2 * ROWS


def inverse_kernel(pieces, inverse, out, scratch, packed):
    scratch[...] = pieces[...].astype(jnp.float32)
    for row in range(ROWS):
        items = []
        for item in range(ITEMS):
            place = (item * ROWS + row) * 2
            halves = [scratch[pl.ds(place + h, N_DEV, stride=PIECES), :] for h in range(2)]
            items.append(jnp.concatenate(halves, axis=1).astype(jnp.bfloat16))
        spectra = jnp.concatenate(items, axis=0)
        field = dot(inverse[...], spectra)
        for half in range(2):
            packed[pl.ds(row * 2 + half, NLON, stride=TILES), :] = field[
                :, half * 128 : (half + 1) * 128
            ]
    out[...] = packed[...].astype(jnp.bfloat16)


def invert(pieces, inverse):
    return pl.pallas_call(
        inverse_kernel,
        out_shape=jax.ShapeDtypeStruct((NLON * TILES, 128), jnp.bfloat16),
        in_specs=[whole()] * 2,
        out_specs=whole(),
        scratch_shapes=[
            pltpu.VMEM((N_DEV * PIECES, 128), jnp.float32),
            pltpu.VMEM((NLON * TILES, 128), jnp.float32),
        ],
        compiler_params=params(48),
        name="invert",
    )(pieces, inverse)


UNPACK_GROUPS = 4


def unpack_kernel(pieces, out, packed):
    packed[...] = pieces[...].astype(jnp.float32)
    for group in range(UNPACK_GROUPS):
        for row in range(ROWS):
            place = group * LON_DEV * TILES + row * 2
            halves = [packed[pl.ds(place + h, LON_DEV, stride=TILES), :] for h in range(2)]
            out[group * ROWS + row] = jnp.concatenate(halves, axis=1).astype(jnp.bfloat16)


def unpack(pieces):
    block = UNPACK_GROUPS * LON_DEV * TILES
    return pl.pallas_call(
        unpack_kernel,
        out_shape=jax.ShapeDtypeStruct((LAT_DEV, LON_DEV, C), jnp.bfloat16),
        grid=(N_LON // UNPACK_GROUPS,),
        in_specs=[pl.BlockSpec((block, 128), lambda g: (g, 0))],
        out_specs=pl.BlockSpec((UNPACK_GROUPS * ROWS, LON_DEV, C), lambda g: (g, 0, 0)),
        scratch_shapes=[pltpu.VMEM((block, 128), jnp.float32)],
        compiler_params=params(32),
        name="unpack",
    )(pieces)


def fourier(item_axis):
    shape = (ITEMS * N_DEV, 1) if item_axis == 0 else (1, ITEMS * N_DEV)
    index = lax.broadcasted_iota(jnp.int32, shape, item_axis)
    device = index % N_DEV
    order = (index // N_DEV) * (L // ITEMS) + device // 2
    part = device % 2
    longitude = lax.broadcasted_iota(
        jnp.int32, (1, NLON) if item_axis == 0 else (NLON, 1), 1 - item_axis
    )
    phase = longitude.astype(jnp.float32) * order.astype(jnp.float32) + 360.0 * part.astype(
        jnp.float32
    )
    phase = phase - 1440.0 * jnp.round(phase * (1.0 / 1440.0))
    angle = (360.0 - jnp.abs(phase)) * (math.pi / 720.0)
    square = angle * angle
    total = -1.0 / 39916800.0
    for term in (1.0 / 362880.0, -1.0 / 5040.0, 1.0 / 120.0, -1.0 / 6.0, 1.0):
        total = total * square + term
    return (total * angle).astype(jnp.bfloat16)


def exchange(values, axes, count):
    pairs = values.reshape(count, values.shape[0] // (2 * count), 2, 128)
    pairs = lax.all_to_all(pairs, axes, split_axis=0, concat_axis=0, tiled=True)
    return pairs.reshape(values.shape)


def regroup(values):
    return lax.all_to_all(values, "lon", split_axis=0, concat_axis=0, tiled=True)


def shards(cube_cells, block_source, block_weight, lift_in, lift_out, spectral):
    lat_index = lax.axis_index("lat")
    lon_index = lax.axis_index("lon")
    chip = lat_index * (N_LON // 2) + lon_index // 2
    odd = lon_index % 2
    far = SRC_DEV - RIM
    across = lax.ppermute(
        lax.dynamic_slice_in_dim(cube_cells, odd * far, RIM, 0),
        "lon",
        [(i, (i + 1) % N_LON if i % 2 else (i - 1) % N_LON) for i in range(N_LON)],
    )
    beside = lax.ppermute(
        lax.dynamic_slice_in_dim(cube_cells, (1 - odd) * far, RIM, 0),
        "lon",
        [(i, i ^ 1) for i in range(N_LON)],
    )
    offsets = (block_source[:, 0, :] - lon_index * SRC_DEV + RIM) % (N_LON * SRC_DEV)
    places = jnp.concatenate(
        [offsets.reshape(LAT_DEV * K), (odd * (RIM + SRC_DEV)).reshape(1).astype(jnp.int32)]
    )
    forward = fourier(0)
    inverse = fourier(1)
    weighted, plain = legendre(chip)
    lift_blocks = jnp.stack(
        [
            jnp.pad(lift_in, ((row * CIN, C - (row + 1) * CIN), (0, 0)))
            for row in range(ROWS)
        ]
    )
    columns = remap(places, across, cube_cells, beside, block_weight)
    columns = exchange(columns, "lon", N_LON)
    spectra = lift(columns, lift_blocks, lift_out, forward, (inverse, weighted, plain))
    spectra = exchange(spectra, ("lat", "lon"), N_DEV)
    analysis = regroup(analyse(spectra, weighted))
    mixed = regroup(mix(analysis, spectral))
    synthesis = exchange(synthesise(mixed, plain), ("lat", "lon"), N_DEV)
    field = exchange(invert(synthesis, inverse), "lon", N_LON)
    return unpack(field)


def solution(mesh):
    in_specs = (
        P(("lat", "lon"), None, None),
        P("lat", "lon", None),
        P("lat", "lon", None, None, None),
        P(),
        P(),
        P("lon", None, None),
    )
    out_specs = P("lat", "lon", None)
    return jax.shard_map(shards, mesh=mesh, in_specs=in_specs, out_specs=out_specs, check_vma=False)
```

```python
import math

import jax
import jax.numpy as jnp
from jax import lax
from jax.experimental import pallas as pl
from jax.experimental.pallas import tpu as pltpu
from jax.sharding import PartitionSpec as P

NLAT = 720
NLON = 1440
L = 384
CIN = 80
C = 256
TILE = 128
K = 4
SRC_DEV = 48
RIM = 24
LAT_DEV = 45
LON_DEV = 90
N_LAT = 16
N_LON = 16
N_DEV = N_LAT * N_LON

ROWS = 3
GROUPS = LAT_DEV // ROWS
ITEMS = 3
PIECES = 2 * ITEMS * ROWS
DEG = L // N_LON
LATS = ROWS * N_DEV
MIB = 1024 * 1024


def params(mib):
    return pltpu.CompilerParams(vmem_limit_bytes=mib * MIB)


def whole():
    return pl.BlockSpec(memory_space=pltpu.VMEM)


def dot(a, b, dims=((1,), (0,))):
    return lax.dot_general(a, b, (dims, ((), ())), preferred_element_type=jnp.float32)


REMAP_STEPS = 4
STEP_GROUPS = N_LON // REMAP_STEPS
GROUP_ROWS = 2 * LON_DEV


def remap_kernel(offsets, across, own, beside, weight, out, tiles, packed):
    step = pl.program_id(0)

    @pl.when(step == 0)
    def _():
        place = offsets[LAT_DEV * K]
        tiles[pl.ds(place, RIM)] = across[...]
        tiles[pl.ds(RIM + SRC_DEV - place, RIM)] = beside[...]
        tiles[RIM : RIM + SRC_DEV] = own[...]

    def store(sub, values):
        for half in range(2):
            packed[pl.ds(sub * GROUP_ROWS + half, LON_DEV, stride=2), :] = values[
                :, half * 128 : (half + 1) * 128
            ]

    def fill(sub):
        columns = []
        for row in range(ROWS):
            base = ((step * STEP_GROUPS + sub) * ROWS + row) * K
            cells = jnp.concatenate([tiles[offsets[base + k]] for k in range(K)], axis=1)
            blocks = jnp.concatenate([weight[sub * ROWS + row, 0, k] for k in range(K)], axis=1)
            columns.append(dot(blocks, cells, ((1,), (1,))))
        columns.append(jnp.zeros((LON_DEV, C - ROWS * CIN), jnp.float32))
        store(sub, jnp.concatenate(columns, axis=1))

    for sub in range(STEP_GROUPS - 1):
        fill(sub)

    @pl.when(step < REMAP_STEPS - 1)
    def _():
        fill(STEP_GROUPS - 1)

    @pl.when(step == REMAP_STEPS - 1)
    def _():
        store(STEP_GROUPS - 1, jnp.zeros((LON_DEV, C), jnp.float32))

    out[...] = packed[...].astype(jnp.bfloat16)


def remap(offsets, across, own, beside, weight):
    return pl.pallas_call(
        remap_kernel,
        out_shape=jax.ShapeDtypeStruct((N_LON * GROUP_ROWS, 128), jnp.bfloat16),
        grid_spec=pltpu.PrefetchScalarGridSpec(
            num_scalar_prefetch=1,
            grid=(REMAP_STEPS,),
            in_specs=[
                pl.BlockSpec((RIM, CIN, TILE), lambda g, o: (0, 0, 0)),
                pl.BlockSpec((SRC_DEV, CIN, TILE), lambda g, o: (0, 0, 0)),
                pl.BlockSpec((RIM, CIN, TILE), lambda g, o: (0, 0, 0)),
                pl.BlockSpec(
                    (STEP_GROUPS * ROWS, 1, K, LON_DEV, TILE), lambda g, o: (g, 0, 0, 0, 0)
                ),
            ],
            out_specs=pl.BlockSpec((STEP_GROUPS * GROUP_ROWS, 128), lambda g, o: (g, 0)),
            scratch_shapes=[
                pltpu.VMEM((RIM + SRC_DEV + RIM, CIN, TILE), jnp.bfloat16),
                pltpu.VMEM((STEP_GROUPS * GROUP_ROWS, 128), jnp.float32),
            ],
        ),
        compiler_params=params(40),
        name="remap",
    )(offsets, across, own, beside, weight)


def lift_kernel(cols, matrices, *rest):
    out, packed, scratch, lifted, first, second, table, sems = rest[-8:]
    first[...] = jnp.zeros_like(first)
    count = ITEMS * N_DEV
    places = [first.at[row, row * CIN : (row + 1) * CIN] for row in range(ROWS)]
    copies = [
        pltpu.make_async_copy(matrices.at[count + C : count + C + CIN, :C], place, sems.at[row])
        for row, place in enumerate(places)
    ]
    copies.append(
        pltpu.make_async_copy(matrices.at[count : count + C, :C], second, sems.at[ROWS])
    )
    copies.append(pltpu.make_async_copy(matrices.at[:count], table, sems.at[ROWS + 1]))
    for copy in copies:
        copy.start()
    packed[...] = cols[...].astype(jnp.float32)
    halves = [packed[pl.ds(h, NLON, stride=2), :] for h in range(2)]
    values = jnp.concatenate(halves, axis=1).astype(jnp.bfloat16)
    for copy in copies[:-1]:
        copy.wait()
    for row in range(ROWS):
        hidden = jax.nn.gelu(dot(values, first[row])).astype(jnp.bfloat16)
        lifted[:, row * C : (row + 1) * C] = dot(hidden, second[...]).astype(jnp.bfloat16)
    copies[-1].wait()
    for item in range(ITEMS):
        spectra = dot(table[item * N_DEV : (item + 1) * N_DEV], lifted[...])
        for piece in range(2 * ROWS):
            scratch[pl.ds(item * 2 * ROWS + piece, N_DEV, stride=PIECES), :] = spectra[
                :, piece * 128 : (piece + 1) * 128
            ]
    out[...] = scratch[...].astype(jnp.bfloat16)


def lift(cols, matrices, tables):
    return pl.pallas_call(
        lift_kernel,
        out_shape=jax.ShapeDtypeStruct((N_DEV * PIECES, 128), jnp.bfloat16),
        in_specs=[whole()] + [pl.BlockSpec(memory_space=pl.ANY)] * (1 + len(tables)),
        out_specs=whole(),
        scratch_shapes=[
            pltpu.VMEM((2 * NLON, 128), jnp.float32),
            pltpu.VMEM((N_DEV * PIECES, 128), jnp.float32),
            pltpu.VMEM((NLON, ROWS * C), jnp.bfloat16),
            pltpu.VMEM((ROWS, C, C), jnp.bfloat16),
            pltpu.VMEM((C, C), jnp.bfloat16),
            pltpu.VMEM((ITEMS * N_DEV, NLON), jnp.bfloat16),
            pltpu.SemaphoreType.DMA((ROWS + 2,)),
        ],
        compiler_params=params(48),
        name="lift",
    )(cols, matrices, *tables)


def legendre_kernel(rise, fall, start, initial, restore, factor, cosine, quad, weighted, plain, table):
    tiles = LATS // 128
    cos = [cosine[:, t * 128 : (t + 1) * 128] for t in range(tiles)]
    init = [initial[:, t * 128 : (t + 1) * 128] for t in range(tiles)]

    def advance(block, carry):
        current, earlier = carry
        for step in range(8):
            degree = block * 8 + step
            up, down, on = rise[degree], fall[degree], start[degree]
            latest = []
            for t in range(tiles):
                value = up * (cos[t] * current[t] - down * earlier[t]) + on * init[t]
                table[t, pl.ds(pl.multiple_of(degree * 8, 8), 8), :] = value
                latest.append(value)
            current, earlier = tuple(latest), current
        return current, earlier

    zero = tuple(jnp.zeros((8, 128), jnp.float32) for _ in range(tiles))
    lax.fori_loop(0, L // 8, advance, (zero, zero))
    for item in range(ITEMS):
        for t in range(tiles):
            lanes = slice(t * 128, (t + 1) * 128)
            values = table[t, pl.ds(item, L, stride=8), :] * restore[item : item + 1, lanes]
            weighted[item, :, lanes] = (values * quad[0:1, lanes]).astype(jnp.bfloat16)
            values = values * factor[item : item + 1, lanes]
            plain[item, lanes, :] = values.T.astype(jnp.bfloat16)


def legendre(chip):
    lane = jnp.arange(LATS, dtype=jnp.int32)
    row, device = lane // N_DEV, lane % N_DEV
    band, group = device // N_LON, device % N_LON
    held = (group < GROUPS)[None, :]
    latitude = band * LAT_DEV + jnp.minimum(group, GROUPS - 1) * ROWS + row
    colatitude = (latitude.astype(jnp.float32) + 0.5) * (math.pi / NLAT)
    cosine = jnp.cos(colatitude)[None, :]
    sine = jnp.sin(colatitude)[None, :]
    slot = jnp.arange(8, dtype=jnp.int32)
    order = (jnp.minimum(slot, ITEMS - 1) * (L // ITEMS) + chip).astype(jnp.float32)
    order_col = order[:, None]
    log_scale = (
        0.5
        * (
            jnp.log(2.0 * order_col + 1.0)
            - math.log(4.0 * math.pi)
            + lax.lgamma(2.0 * order_col + 1.0)
            - 2.0 * lax.lgamma(order_col + 1.0)
            - order_col * math.log(4.0)
        )
        + order_col * jnp.log(sine)
    )
    initial = jnp.exp(jnp.minimum(log_scale + 80.0, 0.0))
    restore = jnp.where(held, jnp.exp(jnp.maximum(log_scale, -80.0)), 0.0)
    quad = jnp.broadcast_to(sine * (math.pi / NLAT) * (2.0 * math.pi / NLON), (8, LATS))
    factor = jnp.broadcast_to(jnp.where(order_col == 0.0, 1.0, 2.0), (8, LATS))
    degree = jnp.arange(L, dtype=jnp.int32).astype(jnp.float32)[:, None, None]
    order_row = order[None, :, None]
    square = degree * degree
    rising = jnp.sqrt(
        jnp.maximum(4.0 * square - 1.0, 1.0) / jnp.maximum(square - order_row * order_row, 1.0)
    )
    shifted = (degree - 1.0) * (degree - 1.0)
    falling = jnp.sqrt(
        jnp.maximum(shifted - order_row * order_row, 0.0) / jnp.maximum(4.0 * shifted - 1.0, 1.0)
    )
    start = jnp.where(degree == order_row, 1.0, 0.0)
    spread = lambda values: jnp.broadcast_to(values, (L, 8, 128))
    return pl.pallas_call(
        legendre_kernel,
        out_shape=(
            jax.ShapeDtypeStruct((ITEMS, L, LATS), jnp.bfloat16),
            jax.ShapeDtypeStruct((ITEMS, LATS, L), jnp.bfloat16),
        ),
        in_specs=[whole()] * 8,
        out_specs=(whole(), whole()),
        scratch_shapes=[pltpu.VMEM((LATS // 128, L * 8, 128), jnp.float32)],
        compiler_params=params(40),
        name="legendre",
    )(
        spread(rising),
        spread(falling),
        spread(start),
        initial,
        restore,
        factor,
        jnp.broadcast_to(cosine, (8, LATS)),
        quad,
    )


def analyse_kernel(pieces, weighted, out, scratch):
    scratch[...] = pieces[...].astype(jnp.float32)
    for item in range(ITEMS):
        rows = []
        for row in range(ROWS):
            place = (item * ROWS + row) * 2
            halves = [scratch[pl.ds(place + h, N_DEV, stride=PIECES), :] for h in range(2)]
            rows.append(jnp.concatenate(halves, axis=1).astype(jnp.bfloat16))
        spectra = jnp.concatenate(rows, axis=0)
        result = dot(weighted[item], spectra).reshape(N_LON, DEG, C)
        out[:, item * DEG : (item + 1) * DEG, :] = result.astype(jnp.bfloat16)


def analyse(pieces, weighted):
    return pl.pallas_call(
        analyse_kernel,
        out_shape=jax.ShapeDtypeStruct((N_LON, ITEMS * DEG, C), jnp.bfloat16),
        in_specs=[whole()] * 2,
        out_specs=whole(),
        scratch_shapes=[pltpu.VMEM((N_DEV * PIECES, 128), jnp.float32)],
        compiler_params=params(40),
        name="analyse",
    )(pieces, weighted)


MIX_STEPS = 4
MIX_DEG = DEG // MIX_STEPS


def mix_kernel(pieces, spectral, out, source, result):
    step = pl.program_id(0)
    count = N_LON * ITEMS

    @pl.when(step == 0)
    def _():
        values = pieces[...].astype(jnp.float32).reshape(count * DEG, C)
        source[0] = values[:, :128]
        source[1] = values[:, 128:]

    for index in range(MIX_DEG):
        degree = step * MIX_DEG + index
        halves = [source[h, pl.ds(degree, count, stride=DEG), :] for h in range(2)]
        values = jnp.concatenate(halves, axis=1).astype(jnp.bfloat16)
        mixed = dot(values, spectral[index])
        for h in range(2):
            result[h, pl.ds(degree, count, stride=DEG), :] = mixed[:, h * 128 : (h + 1) * 128]

    @pl.when(step == MIX_STEPS - 1)
    def _():
        for h in range(2):
            values = result[h].reshape(N_LON, ITEMS * DEG, 128)
            out[:, :, h * 128 : (h + 1) * 128] = values.astype(jnp.bfloat16)


def mix(pieces, spectral):
    shape = (N_LON, ITEMS * DEG, C)
    return pl.pallas_call(
        mix_kernel,
        out_shape=jax.ShapeDtypeStruct(shape, jnp.bfloat16),
        grid=(MIX_STEPS,),
        in_specs=[
            pl.BlockSpec(shape, lambda g: (0, 0, 0)),
            pl.BlockSpec((MIX_DEG, C, C), lambda g: (g, 0, 0)),
        ],
        out_specs=pl.BlockSpec(shape, lambda g: (0, 0, 0)),
        scratch_shapes=[pltpu.VMEM((2, N_LON * ITEMS * DEG, 128), jnp.float32)] * 2,
        compiler_params=params(40),
        name="mix",
    )(pieces, spectral)


def synthesise_kernel(pieces, plain, out, scratch):
    for item in range(ITEMS):
        values = pieces[...].astype(jnp.float32)[:, item * DEG : (item + 1) * DEG, :]
        mixed = values.reshape(L, C).astype(jnp.bfloat16)
        result = dot(plain[item], mixed)
        for row in range(ROWS):
            for half in range(2):
                place = (item * ROWS + row) * 2 + half
                scratch[pl.ds(place, N_DEV, stride=PIECES), :] = result[
                    row * N_DEV : (row + 1) * N_DEV, half * 128 : (half + 1) * 128
                ]
    out[...] = scratch[...].astype(jnp.bfloat16)


def synthesise(pieces, plain):
    return pl.pallas_call(
        synthesise_kernel,
        out_shape=jax.ShapeDtypeStruct((N_DEV * PIECES, 128), jnp.bfloat16),
        in_specs=[whole()] * 2,
        out_specs=whole(),
        scratch_shapes=[pltpu.VMEM((N_DEV * PIECES, 128), jnp.float32)],
        compiler_params=params(40),
        name="synthesise",
    )(pieces, plain)


TILES = 2 * ROWS
INVERT_BLOCK = NLON // 3


def inverse_kernel(pieces, inverse, out, scratch, packed):
    scratch[...] = pieces[...].astype(jnp.float32)
    items = []
    for item in range(ITEMS):
        places = [item * TILES + piece for piece in range(TILES)]
        parts = [scratch[pl.ds(place, N_DEV, stride=PIECES), :] for place in places]
        items.append(jnp.concatenate(parts, axis=1).astype(jnp.bfloat16))
    spectra = jnp.concatenate(items, axis=0)
    for start in range(0, NLON, INVERT_BLOCK):
        field = dot(inverse[start : start + INVERT_BLOCK], spectra)
        for piece in range(TILES):
            packed[pl.ds(start * TILES + piece, INVERT_BLOCK, stride=TILES), :] = field[
                :, piece * 128 : (piece + 1) * 128
            ]
    out[...] = packed[...].astype(jnp.bfloat16)


def invert(pieces, inverse):
    return pl.pallas_call(
        inverse_kernel,
        out_shape=jax.ShapeDtypeStruct((NLON * TILES, 128), jnp.bfloat16),
        in_specs=[whole()] * 2,
        out_specs=whole(),
        scratch_shapes=[
            pltpu.VMEM((N_DEV * PIECES, 128), jnp.float32),
            pltpu.VMEM((NLON * TILES, 128), jnp.float32),
        ],
        compiler_params=params(48),
        name="invert",
    )(pieces, inverse)


UNPACK_GROUPS = 4


def unpack_kernel(pieces, out, packed):
    packed[...] = pieces[...].astype(jnp.float32)
    for group in range(UNPACK_GROUPS):
        for row in range(ROWS):
            place = group * LON_DEV * TILES + row * 2
            halves = [packed[pl.ds(place + h, LON_DEV, stride=TILES), :] for h in range(2)]
            out[group * ROWS + row] = jnp.concatenate(halves, axis=1).astype(jnp.bfloat16)


def unpack(pieces):
    block = UNPACK_GROUPS * LON_DEV * TILES
    return pl.pallas_call(
        unpack_kernel,
        out_shape=jax.ShapeDtypeStruct((LAT_DEV, LON_DEV, C), jnp.bfloat16),
        grid=(N_LON // UNPACK_GROUPS,),
        in_specs=[pl.BlockSpec((block, 128), lambda g: (g, 0))],
        out_specs=pl.BlockSpec((UNPACK_GROUPS * ROWS, LON_DEV, C), lambda g: (g, 0, 0)),
        scratch_shapes=[pltpu.VMEM((block, 128), jnp.float32)],
        compiler_params=params(32),
        name="unpack",
    )(pieces)


def fourier(item_axis, extra=0):
    items = ITEMS * N_DEV + extra
    shape = (items, 1) if item_axis == 0 else (1, items)
    index = lax.broadcasted_iota(jnp.int32, shape, item_axis)
    device = index % N_DEV
    order = (index // N_DEV) * (L // ITEMS) + device // 2
    part = device % 2
    longitude = lax.broadcasted_iota(
        jnp.int32, (1, NLON) if item_axis == 0 else (NLON, 1), 1 - item_axis
    )
    phase = longitude.astype(jnp.float32) * order.astype(jnp.float32) + 360.0 * part.astype(
        jnp.float32
    )
    phase = phase - 1440.0 * jnp.round(phase * (1.0 / 1440.0))
    angle = (360.0 - jnp.abs(phase)) * (math.pi / 720.0)
    square = angle * angle
    total = -1.0 / 39916800.0
    for term in (1.0 / 362880.0, -1.0 / 5040.0, 1.0 / 120.0, -1.0 / 6.0, 1.0):
        total = total * square + term
    return (total * angle).astype(jnp.bfloat16)


def lift_matrices(lift_in, lift_out):
    table = fourier(0, C + CIN)
    rows, wide = table.shape[0], (0, NLON - C)
    below = jnp.pad(lift_out, ((ITEMS * N_DEV, CIN), wide)) + jnp.pad(lift_in, ((rows - CIN, 0), wide))
    index = lax.broadcasted_iota(jnp.int32, (rows, 1), 0)
    return jnp.where(index < ITEMS * N_DEV, table, below)


def exchange(values, axes, count):
    pairs = values.reshape(count, values.shape[0] // (2 * count), 2, 128)
    pairs = lax.all_to_all(pairs, axes, split_axis=0, concat_axis=0, tiled=True)
    return pairs.reshape(values.shape)


def regroup(values):
    return lax.all_to_all(values, "lon", split_axis=0, concat_axis=0, tiled=True)


def shards(cube_cells, block_source, block_weight, lift_in, lift_out, spectral):
    lat_index = lax.axis_index("lat")
    lon_index = lax.axis_index("lon")
    chip = lat_index * (N_LON // 2) + lon_index // 2
    odd = lon_index % 2
    far = SRC_DEV - RIM
    across = lax.ppermute(
        lax.dynamic_slice_in_dim(cube_cells, odd * far, RIM, 0),
        "lon",
        [(i, (i + 1) % N_LON if i % 2 else (i - 1) % N_LON) for i in range(N_LON)],
    )
    beside = lax.ppermute(
        lax.dynamic_slice_in_dim(cube_cells, (1 - odd) * far, RIM, 0),
        "lon",
        [(i, i ^ 1) for i in range(N_LON)],
    )
    offsets = (block_source[:, 0, :] - lon_index * SRC_DEV + RIM) % (N_LON * SRC_DEV)
    places = jnp.concatenate(
        [offsets.reshape(LAT_DEV * K), (odd * (RIM + SRC_DEV)).reshape(1).astype(jnp.int32)]
    )
    matrices = lift_matrices(lift_in, lift_out)
    inverse = fourier(1)
    weighted, plain = legendre(chip)
    columns = remap(places, across, cube_cells, beside, block_weight)
    columns = exchange(columns, "lon", N_LON)
    spectra = lift(columns, matrices, (inverse, weighted, plain))
    spectra = exchange(spectra, ("lat", "lon"), N_DEV)
    analysis = regroup(analyse(spectra, weighted))
    mixed = regroup(mix(analysis, spectral))
    synthesis = exchange(synthesise(mixed, plain), ("lat", "lon"), N_DEV)
    field = exchange(invert(synthesis, inverse), "lon", N_LON)
    return unpack(field)


def solution(mesh):
    in_specs = (
        P(("lat", "lon"), None, None),
        P("lat", "lon", None),
        P("lat", "lon", None, None, None),
        P(),
        P(),
        P("lon", None, None),
    )
    out_specs = P("lat", "lon", None)
    return jax.shard_map(shards, mesh=mesh, in_specs=in_specs, out_specs=out_specs, check_vma=False)
```

```python
import math

import jax
import jax.numpy as jnp
from jax import lax
from jax.experimental import pallas as pl
from jax.experimental.pallas import tpu as pltpu
from jax.sharding import PartitionSpec as P

NLAT = 720
NLON = 1440
L = 384
CIN = 80
C = 256
TILE = 128
K = 4
SRC_DEV = 48
RIM = 24
LAT_DEV = 45
LON_DEV = 90
N_LAT = 16
N_LON = 16
N_DEV = N_LAT * N_LON

ROWS = 3
GROUPS = LAT_DEV // ROWS
ITEMS = 3
PIECES = 2 * ITEMS * ROWS
DEG = L // N_LON
LATS = ROWS * N_DEV
MIB = 1024 * 1024


def params(mib):
    return pltpu.CompilerParams(vmem_limit_bytes=mib * MIB)


def whole():
    return pl.BlockSpec(memory_space=pltpu.VMEM)


def dot(a, b, dims=((1,), (0,))):
    return lax.dot_general(a, b, (dims, ((), ())), preferred_element_type=jnp.float32)


GROUP_ROWS = 2 * LON_DEV


def remap_kernel(offsets, across, own, beside, weight, out, zero, tiles, packed):
    place = offsets[LAT_DEV * K]
    tiles[pl.ds(place, RIM)] = across[...]
    tiles[pl.ds(RIM + SRC_DEV - place, RIM)] = beside[...]
    tiles[RIM : RIM + SRC_DEV] = own[...]
    zero[...] = jnp.zeros_like(zero)
    for group in range(GROUPS):
        columns = []
        for row in range(group * ROWS, (group + 1) * ROWS):
            cells = jnp.concatenate([tiles[offsets[row * K + k]] for k in range(K)], axis=1)
            blocks = jnp.concatenate([weight[row, 0, k] for k in range(K)], axis=1)
            columns.append(dot(blocks, cells, ((1,), (1,))))
        columns.append(jnp.zeros((LON_DEV, C - ROWS * CIN), jnp.float32))
        values = jnp.concatenate(columns, axis=1)
        for half in range(2):
            packed[pl.ds(group * GROUP_ROWS + half, LON_DEV, stride=2), :] = values[
                :, half * 128 : (half + 1) * 128
            ]
    packed[GROUPS * GROUP_ROWS :] = jnp.zeros(((N_LON - GROUPS) * GROUP_ROWS, 128), jnp.float32)
    out[...] = packed[...].astype(jnp.bfloat16)


def remap(offsets, across, own, beside, weight):
    return pl.pallas_call(
        remap_kernel,
        out_shape=(
            jax.ShapeDtypeStruct((N_LON * GROUP_ROWS, 128), jnp.bfloat16),
            jax.ShapeDtypeStruct((8, 128), jnp.float32),
        ),
        grid=(1,),
        in_specs=[pl.BlockSpec(memory_space=pltpu.SMEM)] + [whole()] * 4,
        out_specs=(pl.BlockSpec((N_LON * GROUP_ROWS, 128), lambda g: (0, 0)), whole()),
        scratch_shapes=[
            pltpu.VMEM((RIM + SRC_DEV + RIM, CIN, TILE), jnp.bfloat16),
            pltpu.VMEM((N_LON * GROUP_ROWS, 128), jnp.float32),
        ],
        compiler_params=params(40),
        name="remap",
    )(offsets, across, own, beside, weight)


def lift_kernel(cols, matrices, *rest):
    out, packed, scratch, lifted, first, second, table, sems = rest[-8:]
    first[...] = jnp.zeros_like(first)
    count = ITEMS * N_DEV
    places = [first.at[row, row * CIN : (row + 1) * CIN] for row in range(ROWS)]
    copies = [
        pltpu.make_async_copy(matrices.at[count + C : count + C + CIN, :C], place, sems.at[row])
        for row, place in enumerate(places)
    ]
    copies.append(
        pltpu.make_async_copy(matrices.at[count : count + C, :C], second, sems.at[ROWS])
    )
    for item in range(ITEMS):
        block = pl.ds(item * N_DEV, N_DEV)
        copies.append(
            pltpu.make_async_copy(matrices.at[block], table.at[block], sems.at[ROWS + 1 + item])
        )
    for copy in copies:
        copy.start()
    packed[...] = cols[...].astype(jnp.float32)
    halves = [packed[pl.ds(h, NLON, stride=2), :] for h in range(2)]
    values = jnp.concatenate(halves, axis=1).astype(jnp.bfloat16)
    for copy in copies[: ROWS + 1]:
        copy.wait()
    for row in range(ROWS):
        hidden = jax.nn.gelu(dot(values, first[row])).astype(jnp.bfloat16)
        lifted[:, row * C : (row + 1) * C] = dot(hidden, second[...]).astype(jnp.bfloat16)
    for item in range(ITEMS):
        copies[ROWS + 1 + item].wait()
        spectra = dot(table[item * N_DEV : (item + 1) * N_DEV], lifted[...])
        for piece in range(2 * ROWS):
            scratch[pl.ds(item * 2 * ROWS + piece, N_DEV, stride=PIECES), :] = spectra[
                :, piece * 128 : (piece + 1) * 128
            ]
    out[...] = scratch[...].astype(jnp.bfloat16)


def lift(cols, matrices, tables):
    return pl.pallas_call(
        lift_kernel,
        out_shape=jax.ShapeDtypeStruct((N_DEV * PIECES, 128), jnp.bfloat16),
        in_specs=[whole()] + [pl.BlockSpec(memory_space=pl.ANY)] * (1 + len(tables)),
        out_specs=whole(),
        scratch_shapes=[
            pltpu.VMEM((2 * NLON, 128), jnp.float32),
            pltpu.VMEM((N_DEV * PIECES, 128), jnp.float32),
            pltpu.VMEM((NLON, ROWS * C), jnp.bfloat16),
            pltpu.VMEM((ROWS, C, C), jnp.bfloat16),
            pltpu.VMEM((C, C), jnp.bfloat16),
            pltpu.VMEM((ITEMS * N_DEV, NLON), jnp.bfloat16),
            pltpu.SemaphoreType.DMA((ROWS + 1 + ITEMS,)),
        ],
        compiler_params=params(48),
        name="lift",
    )(cols, matrices, *tables)


def legendre_kernel(
    rise, fall, start, initial, restore, factor, cosine, quad, after, weighted, plain, table
):
    tiles = LATS // 128
    cos = [cosine[:, t * 128 : (t + 1) * 128] for t in range(tiles)]
    init = [initial[:, t * 128 : (t + 1) * 128] for t in range(tiles)]

    def advance(block, carry):
        current, earlier = carry
        for step in range(8):
            degree = block * 8 + step
            up, down, on = rise[degree], fall[degree], start[degree]
            latest = []
            for t in range(tiles):
                value = up * (cos[t] * current[t] - down * earlier[t]) + on * init[t]
                table[t, pl.ds(pl.multiple_of(degree * 8, 8), 8), :] = value
                latest.append(value)
            current, earlier = tuple(latest), current
        return current, earlier

    zero = tuple(jnp.zeros((8, 128), jnp.float32) for _ in range(tiles))
    lax.fori_loop(0, L // 8, advance, (zero, zero))
    for item in range(ITEMS):
        for t in range(tiles):
            lanes = slice(t * 128, (t + 1) * 128)
            values = table[t, pl.ds(item, L, stride=8), :] * restore[item : item + 1, lanes]
            weighted[item, :, lanes] = (values * quad[0:1, lanes]).astype(jnp.bfloat16)
            values = values * factor[item : item + 1, lanes]
            plain[item, lanes, :] = values.T.astype(jnp.bfloat16)


def legendre(chip, after):
    lane = jnp.arange(LATS, dtype=jnp.int32)
    row, device = lane // N_DEV, lane % N_DEV
    band, group = device // N_LON, device % N_LON
    held = (group < GROUPS)[None, :]
    latitude = band * LAT_DEV + jnp.minimum(group, GROUPS - 1) * ROWS + row
    colatitude = (latitude.astype(jnp.float32) + 0.5) * (math.pi / NLAT)
    cosine = jnp.cos(colatitude)[None, :]
    sine = jnp.sin(colatitude)[None, :]
    slot = jnp.arange(8, dtype=jnp.int32)
    order = (jnp.minimum(slot, ITEMS - 1) * (L // ITEMS) + chip).astype(jnp.float32)
    order_col = order[:, None]
    log_scale = (
        0.5
        * (
            jnp.log(2.0 * order_col + 1.0)
            - math.log(4.0 * math.pi)
            + lax.lgamma(2.0 * order_col + 1.0)
            - 2.0 * lax.lgamma(order_col + 1.0)
            - order_col * math.log(4.0)
        )
        + order_col * jnp.log(sine)
    )
    initial = jnp.exp(jnp.minimum(log_scale + 80.0, 0.0))
    restore = jnp.where(held, jnp.exp(jnp.maximum(log_scale, -80.0)), 0.0)
    quad = jnp.broadcast_to(sine * (math.pi / NLAT) * (2.0 * math.pi / NLON), (8, LATS))
    factor = jnp.broadcast_to(jnp.where(order_col == 0.0, 1.0, 2.0), (8, LATS))
    degree = jnp.arange(L, dtype=jnp.int32).astype(jnp.float32)[:, None, None]
    order_row = order[None, :, None]
    square = degree * degree
    rising = jnp.sqrt(
        jnp.maximum(4.0 * square - 1.0, 1.0) / jnp.maximum(square - order_row * order_row, 1.0)
    )
    shifted = (degree - 1.0) * (degree - 1.0)
    falling = jnp.sqrt(
        jnp.maximum(shifted - order_row * order_row, 0.0) / jnp.maximum(4.0 * shifted - 1.0, 1.0)
    )
    start = jnp.where(degree == order_row, 1.0, 0.0)
    spread = lambda values: jnp.broadcast_to(values, (L, 8, 128))
    return pl.pallas_call(
        legendre_kernel,
        out_shape=(
            jax.ShapeDtypeStruct((ITEMS, L, LATS), jnp.bfloat16),
            jax.ShapeDtypeStruct((ITEMS, LATS, L), jnp.bfloat16),
        ),
        in_specs=[whole()] * 8 + [pl.BlockSpec(memory_space=pl.ANY)],
        out_specs=(whole(), whole()),
        scratch_shapes=[pltpu.VMEM((LATS // 128, L * 8, 128), jnp.float32)],
        compiler_params=params(40),
        name="legendre",
    )(
        spread(rising),
        spread(falling),
        spread(start),
        initial,
        restore,
        factor,
        jnp.broadcast_to(cosine, (8, LATS)),
        quad,
        after,
    )


def analyse_kernel(pieces, weighted, out, scratch):
    scratch[...] = pieces[...].astype(jnp.float32)
    for item in range(ITEMS):
        rows = []
        for row in range(ROWS):
            place = (item * ROWS + row) * 2
            halves = [scratch[pl.ds(place + h, N_DEV, stride=PIECES), :] for h in range(2)]
            rows.append(jnp.concatenate(halves, axis=1).astype(jnp.bfloat16))
        spectra = jnp.concatenate(rows, axis=0)
        result = dot(weighted[item], spectra).reshape(N_LON, DEG, C)
        out[:, item * DEG : (item + 1) * DEG, :] = result.astype(jnp.bfloat16)


def analyse(pieces, weighted):
    return pl.pallas_call(
        analyse_kernel,
        out_shape=jax.ShapeDtypeStruct((N_LON, ITEMS * DEG, C), jnp.bfloat16),
        in_specs=[whole()] * 2,
        out_specs=whole(),
        scratch_shapes=[pltpu.VMEM((N_DEV * PIECES, 128), jnp.float32)],
        compiler_params=params(40),
        name="analyse",
    )(pieces, weighted)


def mix_kernel(pieces, spectral, out, source, result):
    count = N_LON * ITEMS
    values = pieces[...].astype(jnp.float32).reshape(count * DEG, C)
    source[0] = values[:, :128]
    source[1] = values[:, 128:]
    for degree in range(DEG):
        halves = [source[h, pl.ds(degree, count, stride=DEG), :] for h in range(2)]
        values = jnp.concatenate(halves, axis=1).astype(jnp.bfloat16)
        mixed = dot(values, spectral[degree])
        for h in range(2):
            result[h, pl.ds(degree, count, stride=DEG), :] = mixed[:, h * 128 : (h + 1) * 128]
    for h in range(2):
        values = result[h].reshape(N_LON, ITEMS * DEG, 128)
        out[:, :, h * 128 : (h + 1) * 128] = values.astype(jnp.bfloat16)


def mix(pieces, spectral):
    return pl.pallas_call(
        mix_kernel,
        out_shape=jax.ShapeDtypeStruct((N_LON, ITEMS * DEG, C), jnp.bfloat16),
        in_specs=[whole()] * 2,
        out_specs=whole(),
        scratch_shapes=[pltpu.VMEM((2, N_LON * ITEMS * DEG, 128), jnp.float32)] * 2,
        compiler_params=params(40),
        name="mix",
    )(pieces, spectral)


def synthesise_kernel(pieces, plain, out, scratch):
    for item in range(ITEMS):
        values = pieces[...].astype(jnp.float32)[:, item * DEG : (item + 1) * DEG, :]
        mixed = values.reshape(L, C).astype(jnp.bfloat16)
        result = dot(plain[item], mixed)
        for row in range(ROWS):
            for half in range(2):
                place = (item * ROWS + row) * 2 + half
                scratch[pl.ds(place, N_DEV, stride=PIECES), :] = result[
                    row * N_DEV : (row + 1) * N_DEV, half * 128 : (half + 1) * 128
                ]
    out[...] = scratch[...].astype(jnp.bfloat16)


def synthesise(pieces, plain):
    return pl.pallas_call(
        synthesise_kernel,
        out_shape=jax.ShapeDtypeStruct((N_DEV * PIECES, 128), jnp.bfloat16),
        in_specs=[whole()] * 2,
        out_specs=whole(),
        scratch_shapes=[pltpu.VMEM((N_DEV * PIECES, 128), jnp.float32)],
        compiler_params=params(40),
        name="synthesise",
    )(pieces, plain)


TILES = 2 * ROWS
INVERT_BLOCK = NLON // 3


def inverse_kernel(pieces, inverse, out, scratch, packed):
    scratch[...] = pieces[...].astype(jnp.float32)
    items = []
    for item in range(ITEMS):
        places = [item * TILES + piece for piece in range(TILES)]
        parts = [scratch[pl.ds(place, N_DEV, stride=PIECES), :] for place in places]
        items.append(jnp.concatenate(parts, axis=1).astype(jnp.bfloat16))
    spectra = jnp.concatenate(items, axis=0)
    for start in range(0, NLON, INVERT_BLOCK):
        field = dot(inverse[start : start + INVERT_BLOCK], spectra)
        for piece in range(TILES):
            packed[pl.ds(start * TILES + piece, INVERT_BLOCK, stride=TILES), :] = field[
                :, piece * 128 : (piece + 1) * 128
            ]
    out[...] = packed[...].astype(jnp.bfloat16)


def invert(pieces, inverse):
    return pl.pallas_call(
        inverse_kernel,
        out_shape=jax.ShapeDtypeStruct((NLON * TILES, 128), jnp.bfloat16),
        in_specs=[whole()] * 2,
        out_specs=whole(),
        scratch_shapes=[
            pltpu.VMEM((N_DEV * PIECES, 128), jnp.float32),
            pltpu.VMEM((NLON * TILES, 128), jnp.float32),
        ],
        compiler_params=params(48),
        name="invert",
    )(pieces, inverse)


UNPACK_GROUPS = 4


def unpack_kernel(pieces, out, packed):
    packed[...] = pieces[...].astype(jnp.float32)
    for group in range(UNPACK_GROUPS):
        for row in range(ROWS):
            place = group * LON_DEV * TILES + row * 2
            halves = [packed[pl.ds(place + h, LON_DEV, stride=TILES), :] for h in range(2)]
            out[group * ROWS + row] = jnp.concatenate(halves, axis=1).astype(jnp.bfloat16)


def unpack(pieces):
    block = UNPACK_GROUPS * LON_DEV * TILES
    return pl.pallas_call(
        unpack_kernel,
        out_shape=jax.ShapeDtypeStruct((LAT_DEV, LON_DEV, C), jnp.bfloat16),
        grid=(N_LON // UNPACK_GROUPS,),
        in_specs=[pl.BlockSpec((block, 128), lambda g: (g, 0))],
        out_specs=pl.BlockSpec((UNPACK_GROUPS * ROWS, LON_DEV, C), lambda g: (g, 0, 0)),
        scratch_shapes=[pltpu.VMEM((block, 128), jnp.float32)],
        compiler_params=params(32),
        name="unpack",
    )(pieces)


def fourier(item_axis, extra=0, shift=0.0):
    items = ITEMS * N_DEV + extra
    shape = (items, 1) if item_axis == 0 else (1, items)
    index = lax.broadcasted_iota(jnp.int32, shape, item_axis)
    device = index % N_DEV
    order = (index // N_DEV) * (L // ITEMS) + device // 2
    part = device % 2
    longitude = lax.broadcasted_iota(
        jnp.int32, (1, NLON) if item_axis == 0 else (NLON, 1), 1 - item_axis
    )
    phase = longitude.astype(jnp.float32) * order.astype(jnp.float32) + 360.0 * part.astype(
        jnp.float32
    )
    phase = phase + shift
    phase = phase - 1440.0 * jnp.round(phase * (1.0 / 1440.0))
    angle = (360.0 - jnp.abs(phase)) * (math.pi / 720.0)
    square = angle * angle
    total = -1.0 / 39916800.0
    for term in (1.0 / 362880.0, -1.0 / 5040.0, 1.0 / 120.0, -1.0 / 6.0, 1.0):
        total = total * square + term
    return (total * angle).astype(jnp.bfloat16)


def lift_matrices(lift_in, lift_out, shift):
    table = fourier(0, C + CIN, shift)
    rows, wide = table.shape[0], (0, NLON - C)
    below = jnp.pad(lift_out, ((ITEMS * N_DEV, CIN), wide)) + jnp.pad(lift_in, ((rows - CIN, 0), wide))
    index = lax.broadcasted_iota(jnp.int32, (rows, 1), 0)
    return jnp.where(index < ITEMS * N_DEV, table, below)


def exchange(values, axes, count):
    pairs = values.reshape(count, values.shape[0] // (2 * count), 2, 128)
    pairs = lax.all_to_all(pairs, axes, split_axis=0, concat_axis=0, tiled=True)
    return pairs.reshape(values.shape)


def regroup(values):
    return lax.all_to_all(values, "lon", split_axis=0, concat_axis=0, tiled=True)


def shards(cube_cells, block_source, block_weight, lift_in, lift_out, spectral):
    lat_index = lax.axis_index("lat")
    lon_index = lax.axis_index("lon")
    chip = lat_index * (N_LON // 2) + lon_index // 2
    odd = lon_index % 2
    far = SRC_DEV - RIM
    across = lax.ppermute(
        lax.dynamic_slice_in_dim(cube_cells, odd * far, RIM, 0),
        "lon",
        [(i, (i + 1) % N_LON if i % 2 else (i - 1) % N_LON) for i in range(N_LON)],
    )
    beside = lax.ppermute(
        lax.dynamic_slice_in_dim(cube_cells, (1 - odd) * far, RIM, 0),
        "lon",
        [(i, i ^ 1) for i in range(N_LON)],
    )
    offsets = (block_source[:, 0, :] - lon_index * SRC_DEV + RIM) % (N_LON * SRC_DEV)
    places = jnp.concatenate(
        [offsets.reshape(LAT_DEV * K), (odd * (RIM + SRC_DEV)).reshape(1).astype(jnp.int32)]
    )
    inverse = fourier(1)
    columns, zero = remap(places, across, cube_cells, beside, block_weight)
    matrices = lift_matrices(lift_in, lift_out, zero[0, 0])
    weighted, plain = legendre(chip, zero)
    columns = exchange(columns, "lon", N_LON)
    spectra = lift(columns, matrices, (inverse, weighted, plain))
    spectra = exchange(spectra, ("lat", "lon"), N_DEV)
    analysis = regroup(analyse(spectra, weighted))
    mixed = regroup(mix(analysis, spectral))
    synthesis = exchange(synthesise(mixed, plain), ("lat", "lon"), N_DEV)
    field = exchange(invert(synthesis, inverse), "lon", N_LON)
    return unpack(field)


def solution(mesh):
    in_specs = (
        P(("lat", "lon"), None, None),
        P("lat", "lon", None),
        P("lat", "lon", None, None, None),
        P(),
        P(),
        P("lon", None, None),
    )
    out_specs = P("lat", "lon", None)
    return jax.shard_map(shards, mesh=mesh, in_specs=in_specs, out_specs=out_specs, check_vma=False)
```

```python
import math

import jax
import jax.numpy as jnp
from jax import lax
from jax.experimental import pallas as pl
from jax.experimental.pallas import tpu as pltpu
from jax.sharding import PartitionSpec as P

NLAT = 720
NLON = 1440
L = 384
CIN = 80
C = 256
TILE = 128
K = 4
SRC_DEV = 48
RIM = 24
LAT_DEV = 45
LON_DEV = 90
N_LAT = 16
N_LON = 16
N_DEV = N_LAT * N_LON

ROWS = 3
GROUPS = LAT_DEV // ROWS
ITEMS = 3
PIECES = 2 * ITEMS * ROWS
DEG = L // N_LON
LATS = ROWS * N_DEV
MIB = 1024 * 1024


def params(mib):
    return pltpu.CompilerParams(vmem_limit_bytes=mib * MIB)


def whole():
    return pl.BlockSpec(memory_space=pltpu.VMEM)


def dot(a, b, dims=((1,), (0,))):
    return lax.dot_general(a, b, (dims, ((), ())), preferred_element_type=jnp.float32)


REMAP_STEPS = 2
STEP_GROUPS = N_LON // REMAP_STEPS
GROUP_ROWS = 2 * LON_DEV


def remap_kernel(offsets, across, own, beside, weight, out, tiles, packed):
    step = pl.program_id(0)

    @pl.when(step == 0)
    def _():
        place = offsets[LAT_DEV * K]
        tiles[pl.ds(place, RIM)] = across[...]
        tiles[pl.ds(RIM + SRC_DEV - place, RIM)] = beside[...]
        tiles[RIM : RIM + SRC_DEV] = own[...]

    def store(sub, values):
        for half in range(2):
            packed[pl.ds(sub * GROUP_ROWS + half, LON_DEV, stride=2), :] = values[
                :, half * 128 : (half + 1) * 128
            ]

    def fill(sub):
        columns = []
        for row in range(ROWS):
            base = ((step * STEP_GROUPS + sub) * ROWS + row) * K
            cells = jnp.concatenate([tiles[offsets[base + k]] for k in range(K)], axis=1)
            blocks = jnp.concatenate([weight[sub * ROWS + row, 0, k] for k in range(K)], axis=1)
            columns.append(dot(blocks, cells, ((1,), (1,))))
        columns.append(jnp.zeros((LON_DEV, C - ROWS * CIN), jnp.float32))
        store(sub, jnp.concatenate(columns, axis=1))

    for sub in range(STEP_GROUPS - 1):
        fill(sub)

    @pl.when(step < REMAP_STEPS - 1)
    def _():
        fill(STEP_GROUPS - 1)

    @pl.when(step == REMAP_STEPS - 1)
    def _():
        store(STEP_GROUPS - 1, jnp.zeros((LON_DEV, C), jnp.float32))

    out[...] = packed[...].astype(jnp.bfloat16)


def remap(offsets, across, own, beside, weight):
    return pl.pallas_call(
        remap_kernel,
        out_shape=jax.ShapeDtypeStruct((N_LON * GROUP_ROWS, 128), jnp.bfloat16),
        grid_spec=pltpu.PrefetchScalarGridSpec(
            num_scalar_prefetch=1,
            grid=(REMAP_STEPS,),
            in_specs=[
                pl.BlockSpec((RIM, CIN, TILE), lambda g, o: (0, 0, 0)),
                pl.BlockSpec((SRC_DEV, CIN, TILE), lambda g, o: (0, 0, 0)),
                pl.BlockSpec((RIM, CIN, TILE), lambda g, o: (0, 0, 0)),
                pl.BlockSpec(
                    (STEP_GROUPS * ROWS, 1, K, LON_DEV, TILE), lambda g, o: (g, 0, 0, 0, 0)
                ),
            ],
            out_specs=pl.BlockSpec((STEP_GROUPS * GROUP_ROWS, 128), lambda g, o: (g, 0)),
            scratch_shapes=[
                pltpu.VMEM((RIM + SRC_DEV + RIM, CIN, TILE), jnp.bfloat16),
                pltpu.VMEM((STEP_GROUPS * GROUP_ROWS, 128), jnp.float32),
            ],
        ),
        compiler_params=params(40),
        name="remap",
    )(offsets, across, own, beside, weight)


def lift_kernel(source, matrices, forward, *rest):
    out, cols, packed, scratch, lifted, first, table, sems = rest[-8:]
    fetch = pltpu.make_async_copy(source, cols, sems.at[0])
    fetch.start()
    copy = pltpu.make_async_copy(forward, table, sems.at[1])
    copy.start()
    first[...] = jnp.zeros_like(first)
    for row in range(ROWS):
        first[row, row * CIN : (row + 1) * CIN] = matrices[C:]
    fetch.wait()
    packed[...] = cols[...].astype(jnp.float32)
    halves = [packed[pl.ds(h, NLON, stride=2), :] for h in range(2)]
    values = jnp.concatenate(halves, axis=1).astype(jnp.bfloat16)
    for row in range(ROWS):
        hidden = jax.nn.gelu(dot(values, first[row])).astype(jnp.bfloat16)
        lifted[:, row * C : (row + 1) * C] = dot(hidden, matrices[:C]).astype(jnp.bfloat16)
    copy.wait()
    for item in range(ITEMS):
        spectra = dot(table[item * N_DEV : (item + 1) * N_DEV], lifted[...])
        for piece in range(2 * ROWS):
            scratch[pl.ds(item * 2 * ROWS + piece, N_DEV, stride=PIECES), :] = spectra[
                :, piece * 128 : (piece + 1) * 128
            ]
    out[...] = scratch[...].astype(jnp.bfloat16)


def lift(cols, matrices, forward, tables):
    return pl.pallas_call(
        lift_kernel,
        out_shape=jax.ShapeDtypeStruct((N_DEV * PIECES, 128), jnp.bfloat16),
        in_specs=[pl.BlockSpec(memory_space=pl.ANY), whole()]
        + [pl.BlockSpec(memory_space=pl.ANY)] * (1 + len(tables)),
        out_specs=whole(),
        scratch_shapes=[
            pltpu.VMEM((2 * NLON, 128), jnp.bfloat16),
            pltpu.VMEM((2 * NLON, 128), jnp.float32),
            pltpu.VMEM((N_DEV * PIECES, 128), jnp.float32),
            pltpu.VMEM((NLON, ROWS * C), jnp.bfloat16),
            pltpu.VMEM((ROWS, C, C), jnp.bfloat16),
            pltpu.VMEM((ITEMS * N_DEV, NLON), jnp.bfloat16),
            pltpu.SemaphoreType.DMA((2,)),
        ],
        compiler_params=params(48),
        name="lift",
    )(cols, matrices, forward, *tables)


def legendre_kernel(rise, fall, start, initial, restore, factor, cosine, quad, weighted, plain, table):
    tiles = LATS // 128
    cos = [cosine[:, t * 128 : (t + 1) * 128] for t in range(tiles)]
    init = [initial[:, t * 128 : (t + 1) * 128] for t in range(tiles)]

    def advance(block, carry):
        current, earlier = carry
        for step in range(8):
            degree = block * 8 + step
            up, down, on = rise[degree], fall[degree], start[degree]
            latest = []
            for t in range(tiles):
                value = up * (cos[t] * current[t] - down * earlier[t]) + on * init[t]
                table[t, pl.ds(pl.multiple_of(degree * 8, 8), 8), :] = value
                latest.append(value)
            current, earlier = tuple(latest), current
        return current, earlier

    zero = tuple(jnp.zeros((8, 128), jnp.float32) for _ in range(tiles))
    lax.fori_loop(0, L // 8, advance, (zero, zero))
    for item in range(ITEMS):
        for t in range(tiles):
            lanes = slice(t * 128, (t + 1) * 128)
            values = table[t, pl.ds(item, L, stride=8), :] * restore[item : item + 1, lanes]
            weighted[item, :, lanes] = (values * quad[0:1, lanes]).astype(jnp.bfloat16)
            values = values * factor[item : item + 1, lanes]
            plain[item, lanes, :] = values.T.astype(jnp.bfloat16)


def legendre(chip):
    lane = jnp.arange(LATS, dtype=jnp.int32)
    row, device = lane // N_DEV, lane % N_DEV
    band, group = device // N_LON, device % N_LON
    held = (group < GROUPS)[None, :]
    latitude = band * LAT_DEV + jnp.minimum(group, GROUPS - 1) * ROWS + row
    colatitude = (latitude.astype(jnp.float32) + 0.5) * (math.pi / NLAT)
    cosine = jnp.cos(colatitude)[None, :]
    sine = jnp.sin(colatitude)[None, :]
    slot = jnp.arange(8, dtype=jnp.int32)
    order = (jnp.minimum(slot, ITEMS - 1) * (L // ITEMS) + chip).astype(jnp.float32)
    order_col = order[:, None]
    log_scale = (
        0.5
        * (
            jnp.log(2.0 * order_col + 1.0)
            - math.log(4.0 * math.pi)
            + lax.lgamma(2.0 * order_col + 1.0)
            - 2.0 * lax.lgamma(order_col + 1.0)
            - order_col * math.log(4.0)
        )
        + order_col * jnp.log(sine)
    )
    initial = jnp.exp(jnp.minimum(log_scale + 80.0, 0.0))
    restore = jnp.where(held, jnp.exp(jnp.maximum(log_scale, -80.0)), 0.0)
    quad = jnp.broadcast_to(sine * (math.pi / NLAT) * (2.0 * math.pi / NLON), (8, LATS))
    factor = jnp.broadcast_to(jnp.where(order_col == 0.0, 1.0, 2.0), (8, LATS))
    degree = jnp.arange(L, dtype=jnp.int32).astype(jnp.float32)[:, None, None]
    order_row = order[None, :, None]
    square = degree * degree
    rising = jnp.sqrt(
        jnp.maximum(4.0 * square - 1.0, 1.0) / jnp.maximum(square - order_row * order_row, 1.0)
    )
    shifted = (degree - 1.0) * (degree - 1.0)
    falling = jnp.sqrt(
        jnp.maximum(shifted - order_row * order_row, 0.0) / jnp.maximum(4.0 * shifted - 1.0, 1.0)
    )
    start = jnp.where(degree == order_row, 1.0, 0.0)
    spread = lambda values: jnp.broadcast_to(values, (L, 8, 128))
    return pl.pallas_call(
        legendre_kernel,
        out_shape=(
            jax.ShapeDtypeStruct((ITEMS, L, LATS), jnp.bfloat16),
            jax.ShapeDtypeStruct((ITEMS, LATS, L), jnp.bfloat16),
        ),
        in_specs=[whole()] * 8,
        out_specs=(whole(), whole()),
        scratch_shapes=[pltpu.VMEM((LATS // 128, L * 8, 128), jnp.float32)],
        compiler_params=params(40),
        name="legendre",
    )(
        spread(rising),
        spread(falling),
        spread(start),
        initial,
        restore,
        factor,
        jnp.broadcast_to(cosine, (8, LATS)),
        quad,
    )


def analyse_kernel(pieces, weighted, out, scratch):
    scratch[...] = pieces[...].astype(jnp.float32)
    for item in range(ITEMS):
        rows = []
        for row in range(ROWS):
            place = (item * ROWS + row) * 2
            halves = [scratch[pl.ds(place + h, N_DEV, stride=PIECES), :] for h in range(2)]
            rows.append(jnp.concatenate(halves, axis=1).astype(jnp.bfloat16))
        spectra = jnp.concatenate(rows, axis=0)
        result = dot(weighted[item], spectra).reshape(N_LON, DEG, C)
        out[:, item * DEG : (item + 1) * DEG, :] = result.astype(jnp.bfloat16)


def analyse(pieces, weighted):
    return pl.pallas_call(
        analyse_kernel,
        out_shape=jax.ShapeDtypeStruct((N_LON, ITEMS * DEG, C), jnp.bfloat16),
        in_specs=[whole()] * 2,
        out_specs=whole(),
        scratch_shapes=[pltpu.VMEM((N_DEV * PIECES, 128), jnp.float32)],
        compiler_params=params(40),
        name="analyse",
    )(pieces, weighted)


def mix_kernel(pieces, spectral, out, source, result):
    count = N_LON * ITEMS
    values = pieces[...].astype(jnp.float32).reshape(count * DEG, C)
    source[0] = values[:, :128]
    source[1] = values[:, 128:]
    for degree in range(DEG):
        halves = [source[h, pl.ds(degree, count, stride=DEG), :] for h in range(2)]
        values = jnp.concatenate(halves, axis=1).astype(jnp.bfloat16)
        mixed = dot(values, spectral[degree])
        for h in range(2):
            result[h, pl.ds(degree, count, stride=DEG), :] = mixed[:, h * 128 : (h + 1) * 128]
    for h in range(2):
        values = result[h].reshape(N_LON, ITEMS * DEG, 128)
        out[:, :, h * 128 : (h + 1) * 128] = values.astype(jnp.bfloat16)


def mix(pieces, spectral):
    return pl.pallas_call(
        mix_kernel,
        out_shape=jax.ShapeDtypeStruct((N_LON, ITEMS * DEG, C), jnp.bfloat16),
        in_specs=[whole()] * 2,
        out_specs=whole(),
        scratch_shapes=[pltpu.VMEM((2, N_LON * ITEMS * DEG, 128), jnp.float32)] * 2,
        compiler_params=params(40),
        name="mix",
    )(pieces, spectral)


def synthesise_kernel(pieces, plain, out, scratch):
    for item in range(ITEMS):
        values = pieces[...].astype(jnp.float32)[:, item * DEG : (item + 1) * DEG, :]
        mixed = values.reshape(L, C).astype(jnp.bfloat16)
        result = dot(plain[item], mixed)
        for row in range(ROWS):
            for half in range(2):
                place = (item * ROWS + row) * 2 + half
                scratch[pl.ds(place, N_DEV, stride=PIECES), :] = result[
                    row * N_DEV : (row + 1) * N_DEV, half * 128 : (half + 1) * 128
                ]
    out[...] = scratch[...].astype(jnp.bfloat16)


def synthesise(pieces, plain):
    return pl.pallas_call(
        synthesise_kernel,
        out_shape=jax.ShapeDtypeStruct((N_DEV * PIECES, 128), jnp.bfloat16),
        in_specs=[whole()] * 2,
        out_specs=whole(),
        scratch_shapes=[pltpu.VMEM((N_DEV * PIECES, 128), jnp.float32)],
        compiler_params=params(40),
        name="synthesise",
    )(pieces, plain)


TILES = 2 * ROWS
INVERT_BLOCK = NLON // 3


def inverse_kernel(pieces, inverse, out, scratch, packed):
    scratch[...] = pieces[...].astype(jnp.float32)
    items = []
    for item in range(ITEMS):
        places = [item * TILES + piece for piece in range(TILES)]
        parts = [scratch[pl.ds(place, N_DEV, stride=PIECES), :] for place in places]
        items.append(jnp.concatenate(parts, axis=1).astype(jnp.bfloat16))
    spectra = jnp.concatenate(items, axis=0)
    for start in range(0, NLON, INVERT_BLOCK):
        field = dot(inverse[start : start + INVERT_BLOCK], spectra)
        for piece in range(TILES):
            packed[pl.ds(start * TILES + piece, INVERT_BLOCK, stride=TILES), :] = field[
                :, piece * 128 : (piece + 1) * 128
            ]
    out[...] = packed[...].astype(jnp.bfloat16)


def invert(pieces, inverse):
    return pl.pallas_call(
        inverse_kernel,
        out_shape=jax.ShapeDtypeStruct((NLON * TILES, 128), jnp.bfloat16),
        in_specs=[whole()] * 2,
        out_specs=whole(),
        scratch_shapes=[
            pltpu.VMEM((N_DEV * PIECES, 128), jnp.float32),
            pltpu.VMEM((NLON * TILES, 128), jnp.float32),
        ],
        compiler_params=params(48),
        name="invert",
    )(pieces, inverse)


UNPACK_GROUPS = 4


def unpack_kernel(pieces, out, packed):
    packed[...] = pieces[...].astype(jnp.float32)
    for group in range(UNPACK_GROUPS):
        for row in range(ROWS):
            place = group * LON_DEV * TILES + row * 2
            halves = [packed[pl.ds(place + h, LON_DEV, stride=TILES), :] for h in range(2)]
            out[group * ROWS + row] = jnp.concatenate(halves, axis=1).astype(jnp.bfloat16)


def unpack(pieces):
    block = UNPACK_GROUPS * LON_DEV * TILES
    return pl.pallas_call(
        unpack_kernel,
        out_shape=jax.ShapeDtypeStruct((LAT_DEV, LON_DEV, C), jnp.bfloat16),
        grid=(N_LON // UNPACK_GROUPS,),
        in_specs=[pl.BlockSpec((block, 128), lambda g: (g, 0))],
        out_specs=pl.BlockSpec((UNPACK_GROUPS * ROWS, LON_DEV, C), lambda g: (g, 0, 0)),
        scratch_shapes=[pltpu.VMEM((block, 128), jnp.float32)],
        compiler_params=params(32),
        name="unpack",
    )(pieces)


def fourier(item_axis):
    shape = (ITEMS * N_DEV, 1) if item_axis == 0 else (1, ITEMS * N_DEV)
    index = lax.broadcasted_iota(jnp.int32, shape, item_axis)
    device = index % N_DEV
    order = (index // N_DEV) * (L // ITEMS) + device // 2
    part = device % 2
    longitude = lax.broadcasted_iota(
        jnp.int32, (1, NLON) if item_axis == 0 else (NLON, 1), 1 - item_axis
    )
    phase = longitude.astype(jnp.float32) * order.astype(jnp.float32) + 360.0 * part.astype(
        jnp.float32
    )
    phase = phase - 1440.0 * jnp.round(phase * (1.0 / 1440.0))
    angle = (360.0 - jnp.abs(phase)) * (math.pi / 720.0)
    square = angle * angle
    total = -1.0 / 39916800.0
    for term in (1.0 / 362880.0, -1.0 / 5040.0, 1.0 / 120.0, -1.0 / 6.0, 1.0):
        total = total * square + term
    return (total * angle).astype(jnp.bfloat16)


def exchange(values, axes, count):
    pairs = values.reshape(count, values.shape[0] // (2 * count), 2, 128)
    pairs = lax.all_to_all(pairs, axes, split_axis=0, concat_axis=0, tiled=True)
    return pairs.reshape(values.shape)


def regroup(values):
    return lax.all_to_all(values, "lon", split_axis=0, concat_axis=0, tiled=True)


def shards(cube_cells, block_source, block_weight, lift_in, lift_out, spectral):
    lat_index = lax.axis_index("lat")
    lon_index = lax.axis_index("lon")
    chip = lat_index * (N_LON // 2) + lon_index // 2
    odd = lon_index % 2
    far = SRC_DEV - RIM
    across = lax.ppermute(
        lax.dynamic_slice_in_dim(cube_cells, odd * far, RIM, 0),
        "lon",
        [(i, (i + 1) % N_LON if i % 2 else (i - 1) % N_LON) for i in range(N_LON)],
    )
    beside = lax.ppermute(
        lax.dynamic_slice_in_dim(cube_cells, (1 - odd) * far, RIM, 0),
        "lon",
        [(i, i ^ 1) for i in range(N_LON)],
    )
    offsets = (block_source[:, 0, :] - lon_index * SRC_DEV + RIM) % (N_LON * SRC_DEV)
    places = jnp.concatenate(
        [offsets.reshape(LAT_DEV * K), (odd * (RIM + SRC_DEV)).reshape(1).astype(jnp.int32)]
    )
    forward = fourier(0)
    matrices = jnp.concatenate([lift_out, lift_in], axis=0)
    inverse = fourier(1)
    weighted, plain = legendre(chip)
    columns = remap(places, across, cube_cells, beside, block_weight)
    columns = exchange(columns, "lon", N_LON)
    spectra = lift(columns, matrices, forward, (inverse, weighted, plain))
    spectra = exchange(spectra, ("lat", "lon"), N_DEV)
    analysis = regroup(analyse(spectra, weighted))
    mixed = regroup(mix(analysis, spectral))
    synthesis = exchange(synthesise(mixed, plain), ("lat", "lon"), N_DEV)
    field = exchange(invert(synthesis, inverse), "lon", N_LON)
    return unpack(field)


def solution(mesh):
    in_specs = (
        P(("lat", "lon"), None, None),
        P("lat", "lon", None),
        P("lat", "lon", None, None, None),
        P(),
        P(),
        P("lon", None, None),
    )
    out_specs = P("lat", "lon", None)
    return jax.shard_map(shards, mesh=mesh, in_specs=in_specs, out_specs=out_specs, check_vma=False)
```

```python
import math

import jax
import jax.numpy as jnp
from jax import lax
from jax.experimental import pallas as pl
from jax.experimental.pallas import tpu as pltpu
from jax.sharding import PartitionSpec as P

NLAT = 720
NLON = 1440
L = 384
CIN = 80
C = 256
TILE = 128
K = 4
SRC_DEV = 48
RIM = 24
LAT_DEV = 45
LON_DEV = 90
N_LAT = 16
N_LON = 16
N_DEV = N_LAT * N_LON

ROWS = 3
GROUPS = LAT_DEV // ROWS
ITEMS = 3
PIECES = 2 * ITEMS * ROWS
DEG = L // N_LON
LATS = ROWS * N_DEV
MIB = 1024 * 1024


def params(mib):
    return pltpu.CompilerParams(vmem_limit_bytes=mib * MIB)


def whole():
    return pl.BlockSpec(memory_space=pltpu.VMEM)


def dot(a, b, dims=((1,), (0,))):
    return lax.dot_general(a, b, (dims, ((), ())), preferred_element_type=jnp.float32)


REMAP_STEPS = 2
STEP_GROUPS = N_LON // REMAP_STEPS
GROUP_ROWS = 2 * LON_DEV


def remap_kernel(offsets, across, own, beside, weight, out, tiles, packed):
    step = pl.program_id(0)

    @pl.when(step == 0)
    def _():
        place = offsets[LAT_DEV * K]
        tiles[pl.ds(place, RIM)] = across[...]
        tiles[pl.ds(RIM + SRC_DEV - place, RIM)] = beside[...]
        tiles[RIM : RIM + SRC_DEV] = own[...]

    def store(sub, values):
        for half in range(2):
            packed[pl.ds(sub * GROUP_ROWS + half, LON_DEV, stride=2), :] = values[
                :, half * 128 : (half + 1) * 128
            ]

    def fill(sub):
        columns = []
        for row in range(ROWS):
            base = ((step * STEP_GROUPS + sub) * ROWS + row) * K
            cells = jnp.concatenate([tiles[offsets[base + k]] for k in range(K)], axis=1)
            blocks = jnp.concatenate([weight[sub * ROWS + row, 0, k] for k in range(K)], axis=1)
            columns.append(dot(blocks, cells, ((1,), (1,))))
        columns.append(jnp.zeros((LON_DEV, C - ROWS * CIN), jnp.float32))
        store(sub, jnp.concatenate(columns, axis=1))

    for sub in range(STEP_GROUPS - 1):
        fill(sub)

    @pl.when(step < REMAP_STEPS - 1)
    def _():
        fill(STEP_GROUPS - 1)

    @pl.when(step == REMAP_STEPS - 1)
    def _():
        store(STEP_GROUPS - 1, jnp.zeros((LON_DEV, C), jnp.float32))

    out[...] = packed[...].astype(jnp.bfloat16)


def remap(offsets, across, own, beside, weight):
    return pl.pallas_call(
        remap_kernel,
        out_shape=jax.ShapeDtypeStruct((N_LON * GROUP_ROWS, 128), jnp.bfloat16),
        grid_spec=pltpu.PrefetchScalarGridSpec(
            num_scalar_prefetch=1,
            grid=(REMAP_STEPS,),
            in_specs=[
                pl.BlockSpec((RIM, CIN, TILE), lambda g, o: (0, 0, 0)),
                pl.BlockSpec((SRC_DEV, CIN, TILE), lambda g, o: (0, 0, 0)),
                pl.BlockSpec((RIM, CIN, TILE), lambda g, o: (0, 0, 0)),
                pl.BlockSpec(
                    (STEP_GROUPS * ROWS, 1, K, LON_DEV, TILE), lambda g, o: (g, 0, 0, 0, 0)
                ),
            ],
            out_specs=pl.BlockSpec((STEP_GROUPS * GROUP_ROWS, 128), lambda g, o: (g, 0)),
            scratch_shapes=[
                pltpu.VMEM((RIM + SRC_DEV + RIM, CIN, TILE), jnp.bfloat16),
                pltpu.VMEM((STEP_GROUPS * GROUP_ROWS, 128), jnp.float32),
            ],
        ),
        compiler_params=params(40),
        name="remap",
    )(offsets, across, own, beside, weight)


def lift_kernel(source, matrices, forward, *rest):
    out, cols, packed, scratch, lifted, first, table, sems = rest[-8:]
    fetch = pltpu.make_async_copy(source, cols, sems.at[0])
    fetch.start()
    copy = pltpu.make_async_copy(forward, table, sems.at[1])
    copy.start()
    first[...] = jnp.zeros_like(first)
    for row in range(ROWS):
        first[row, row * CIN : (row + 1) * CIN] = matrices[C:]
    fetch.wait()
    packed[...] = cols[...].astype(jnp.float32)
    halves = [packed[pl.ds(h, NLON, stride=2), :] for h in range(2)]
    values = jnp.concatenate(halves, axis=1).astype(jnp.bfloat16)
    for row in range(ROWS):
        hidden = jax.nn.gelu(dot(values, first[row])).astype(jnp.bfloat16)
        lifted[:, row * C : (row + 1) * C] = dot(hidden, matrices[:C]).astype(jnp.bfloat16)
    copy.wait()
    for item in range(ITEMS):
        spectra = dot(table[item * N_DEV : (item + 1) * N_DEV], lifted[...])
        for piece in range(2 * ROWS):
            scratch[pl.ds(item * 2 * ROWS + piece, N_DEV, stride=PIECES), :] = spectra[
                :, piece * 128 : (piece + 1) * 128
            ]
    out[...] = scratch[...].astype(jnp.bfloat16)


def lift(cols, matrices, forward, tables):
    return pl.pallas_call(
        lift_kernel,
        out_shape=jax.ShapeDtypeStruct((N_DEV * PIECES, 128), jnp.bfloat16),
        in_specs=[pl.BlockSpec(memory_space=pl.ANY), whole()]
        + [pl.BlockSpec(memory_space=pl.ANY)] * (1 + len(tables)),
        out_specs=whole(),
        scratch_shapes=[
            pltpu.VMEM((2 * NLON, 128), jnp.bfloat16),
            pltpu.VMEM((2 * NLON, 128), jnp.float32),
            pltpu.VMEM((N_DEV * PIECES, 128), jnp.float32),
            pltpu.VMEM((NLON, ROWS * C), jnp.bfloat16),
            pltpu.VMEM((ROWS, C, C), jnp.bfloat16),
            pltpu.VMEM((ITEMS * N_DEV, NLON), jnp.bfloat16),
            pltpu.SemaphoreType.DMA((2,)),
        ],
        compiler_params=params(48),
        name="lift",
    )(cols, matrices, forward, *tables)


def legendre_kernel(rise, fall, start, initial, restore, factor, cosine, quad, weighted, plain, table):
    tiles = LATS // 128
    cos = [cosine[:, t * 128 : (t + 1) * 128] for t in range(tiles)]
    init = [initial[:, t * 128 : (t + 1) * 128] for t in range(tiles)]

    def advance(block, carry):
        current, earlier = carry
        for step in range(8):
            degree = block * 8 + step
            up, down, on = rise[degree], fall[degree], start[degree]
            latest = []
            for t in range(tiles):
                value = up * (cos[t] * current[t] - down * earlier[t]) + on * init[t]
                table[t, pl.ds(pl.multiple_of(degree * 8, 8), 8), :] = value
                latest.append(value)
            current, earlier = tuple(latest), current
        return current, earlier

    zero = tuple(jnp.zeros((8, 128), jnp.float32) for _ in range(tiles))
    lax.fori_loop(0, L // 8, advance, (zero, zero))
    for item in range(ITEMS):
        for t in range(tiles):
            lanes = slice(t * 128, (t + 1) * 128)
            values = table[t, pl.ds(item, L, stride=8), :] * restore[item : item + 1, lanes]
            weighted[item, :, lanes] = (values * quad[0:1, lanes]).astype(jnp.bfloat16)
            values = values * factor[item : item + 1, lanes]
            plain[item, lanes, :] = values.T.astype(jnp.bfloat16)


def legendre(chip):
    lane = jnp.arange(LATS, dtype=jnp.int32)
    row, device = lane // N_DEV, lane % N_DEV
    band, group = device // N_LON, device % N_LON
    held = (group < GROUPS)[None, :]
    latitude = band * LAT_DEV + jnp.minimum(group, GROUPS - 1) * ROWS + row
    colatitude = (latitude.astype(jnp.float32) + 0.5) * (math.pi / NLAT)
    cosine = jnp.cos(colatitude)[None, :]
    sine = jnp.sin(colatitude)[None, :]
    slot = jnp.arange(8, dtype=jnp.int32)
    order = (jnp.minimum(slot, ITEMS - 1) * (L // ITEMS) + chip).astype(jnp.float32)
    order_col = order[:, None]
    log_scale = (
        0.5
        * (
            jnp.log(2.0 * order_col + 1.0)
            - math.log(4.0 * math.pi)
            + lax.lgamma(2.0 * order_col + 1.0)
            - 2.0 * lax.lgamma(order_col + 1.0)
            - order_col * math.log(4.0)
        )
        + order_col * jnp.log(sine)
    )
    initial = jnp.exp(jnp.minimum(log_scale + 80.0, 0.0))
    restore = jnp.where(held, jnp.exp(jnp.maximum(log_scale, -80.0)), 0.0)
    quad = jnp.broadcast_to(sine * (math.pi / NLAT) * (2.0 * math.pi / NLON), (8, LATS))
    factor = jnp.broadcast_to(jnp.where(order_col == 0.0, 1.0, 2.0), (8, LATS))
    degree = jnp.arange(L, dtype=jnp.int32).astype(jnp.float32)[:, None, None]
    order_row = order[None, :, None]
    square = degree * degree
    rising = jnp.sqrt(
        jnp.maximum(4.0 * square - 1.0, 1.0) / jnp.maximum(square - order_row * order_row, 1.0)
    )
    shifted = (degree - 1.0) * (degree - 1.0)
    falling = jnp.sqrt(
        jnp.maximum(shifted - order_row * order_row, 0.0) / jnp.maximum(4.0 * shifted - 1.0, 1.0)
    )
    start = jnp.where(degree == order_row, 1.0, 0.0)
    spread = lambda values: jnp.broadcast_to(values, (L, 8, 128))
    return pl.pallas_call(
        legendre_kernel,
        out_shape=(
            jax.ShapeDtypeStruct((ITEMS, L, LATS), jnp.bfloat16),
            jax.ShapeDtypeStruct((ITEMS, LATS, L), jnp.bfloat16),
        ),
        in_specs=[whole()] * 8,
        out_specs=(whole(), whole()),
        scratch_shapes=[pltpu.VMEM((LATS // 128, L * 8, 128), jnp.float32)],
        compiler_params=params(40),
        name="legendre",
    )(
        spread(rising),
        spread(falling),
        spread(start),
        initial,
        restore,
        factor,
        jnp.broadcast_to(cosine, (8, LATS)),
        quad,
    )


def analyse_kernel(pieces, weighted, out, scratch):
    scratch[...] = pieces[...].astype(jnp.float32)
    for item in range(ITEMS):
        rows = []
        for row in range(ROWS):
            place = (item * ROWS + row) * 2
            halves = [scratch[pl.ds(place + h, N_DEV, stride=PIECES), :] for h in range(2)]
            rows.append(jnp.concatenate(halves, axis=1).astype(jnp.bfloat16))
        spectra = jnp.concatenate(rows, axis=0)
        result = dot(weighted[item], spectra).reshape(N_LON, DEG, C)
        out[:, item * DEG : (item + 1) * DEG, :] = result.astype(jnp.bfloat16)


def analyse(pieces, weighted):
    return pl.pallas_call(
        analyse_kernel,
        out_shape=jax.ShapeDtypeStruct((N_LON, ITEMS * DEG, C), jnp.bfloat16),
        in_specs=[whole()] * 2,
        out_specs=whole(),
        scratch_shapes=[pltpu.VMEM((N_DEV * PIECES, 128), jnp.float32)],
        compiler_params=params(40),
        name="analyse",
    )(pieces, weighted)


def mix_kernel(pieces, spectral, out, source, result):
    count = N_LON * ITEMS
    values = pieces[...].astype(jnp.float32).reshape(count * DEG, C)
    source[0] = values[:, :128]
    source[1] = values[:, 128:]
    for degree in range(DEG):
        halves = [source[h, pl.ds(degree, count, stride=DEG), :] for h in range(2)]
        values = jnp.concatenate(halves, axis=1).astype(jnp.bfloat16)
        mixed = dot(values, spectral[degree])
        for h in range(2):
            result[h, pl.ds(degree, count, stride=DEG), :] = mixed[:, h * 128 : (h + 1) * 128]
    for h in range(2):
        values = result[h].reshape(N_LON, ITEMS * DEG, 128)
        out[:, :, h * 128 : (h + 1) * 128] = values.astype(jnp.bfloat16)


def mix(pieces, spectral):
    return pl.pallas_call(
        mix_kernel,
        out_shape=jax.ShapeDtypeStruct((N_LON, ITEMS * DEG, C), jnp.bfloat16),
        in_specs=[whole()] * 2,
        out_specs=whole(),
        scratch_shapes=[pltpu.VMEM((2, N_LON * ITEMS * DEG, 128), jnp.float32)] * 2,
        compiler_params=params(40),
        name="mix",
    )(pieces, spectral)


def synthesise_kernel(pieces, plain, out, scratch):
    for item in range(ITEMS):
        values = pieces[...].astype(jnp.float32)[:, item * DEG : (item + 1) * DEG, :]
        mixed = values.reshape(L, C).astype(jnp.bfloat16)
        result = dot(plain[item], mixed)
        for row in range(ROWS):
            for half in range(2):
                place = (item * ROWS + row) * 2 + half
                scratch[pl.ds(place, N_DEV, stride=PIECES), :] = result[
                    row * N_DEV : (row + 1) * N_DEV, half * 128 : (half + 1) * 128
                ]
    out[...] = scratch[...].astype(jnp.bfloat16)


def synthesise(pieces, plain):
    return pl.pallas_call(
        synthesise_kernel,
        out_shape=jax.ShapeDtypeStruct((N_DEV * PIECES, 128), jnp.bfloat16),
        in_specs=[whole()] * 2,
        out_specs=whole(),
        scratch_shapes=[pltpu.VMEM((N_DEV * PIECES, 128), jnp.float32)],
        compiler_params=params(40),
        name="synthesise",
    )(pieces, plain)


TILES = 2 * ROWS
INVERT_BLOCK = NLON // 3


def inverse_kernel(pieces, inverse, out, scratch, packed):
    scratch[...] = pieces[...].astype(jnp.float32)
    items = []
    for item in range(ITEMS):
        places = [item * TILES + piece for piece in range(TILES)]
        parts = [scratch[pl.ds(place, N_DEV, stride=PIECES), :] for place in places]
        items.append(jnp.concatenate(parts, axis=1).astype(jnp.bfloat16))
    spectra = jnp.concatenate(items, axis=0)
    for start in range(0, NLON, INVERT_BLOCK):
        field = dot(inverse[start : start + INVERT_BLOCK], spectra)
        for piece in range(TILES):
            packed[pl.ds(start * TILES + piece, INVERT_BLOCK, stride=TILES), :] = field[
                :, piece * 128 : (piece + 1) * 128
            ]
    out[...] = packed[...].astype(jnp.bfloat16)


def invert(pieces, inverse):
    return pl.pallas_call(
        inverse_kernel,
        out_shape=jax.ShapeDtypeStruct((NLON * TILES, 128), jnp.bfloat16),
        in_specs=[whole()] * 2,
        out_specs=whole(),
        scratch_shapes=[
            pltpu.VMEM((N_DEV * PIECES, 128), jnp.float32),
            pltpu.VMEM((NLON * TILES, 128), jnp.float32),
        ],
        compiler_params=params(48),
        name="invert",
    )(pieces, inverse)


UNPACK_PARTS = 5


def unpack_kernel(pieces, out, packed, rows, sems):
    count = GROUPS // UNPACK_PARTS
    size = count * LON_DEV * TILES
    copies = []
    for part in range(UNPACK_PARTS):
        packed[...] = pieces[part * size : (part + 1) * size].astype(jnp.float32)
        for row in range(count * ROWS):
            place = row // ROWS * LON_DEV * TILES + row % ROWS * 2
            halves = [packed[pl.ds(place + h, LON_DEV, stride=TILES), :] for h in range(2)]
            rows[part, row] = jnp.concatenate(halves, axis=1).astype(jnp.bfloat16)
        block = pl.ds(part * count * ROWS, count * ROWS)
        copies.append(pltpu.make_async_copy(rows.at[part], out.at[block], sems.at[part]))
        copies[-1].start()
    for copy in copies:
        copy.wait()


def unpack(pieces):
    count = GROUPS // UNPACK_PARTS
    return pl.pallas_call(
        unpack_kernel,
        out_shape=jax.ShapeDtypeStruct((LAT_DEV, LON_DEV, C), jnp.bfloat16),
        in_specs=[whole()],
        out_specs=pl.BlockSpec(memory_space=pl.ANY),
        scratch_shapes=[
            pltpu.VMEM((count * LON_DEV * TILES, 128), jnp.float32),
            pltpu.VMEM((UNPACK_PARTS, count * ROWS, LON_DEV, C), jnp.bfloat16),
            pltpu.SemaphoreType.DMA((UNPACK_PARTS,)),
        ],
        compiler_params=params(32),
        name="unpack",
    )(pieces)


def fourier(item_axis):
    shape = (ITEMS * N_DEV, 1) if item_axis == 0 else (1, ITEMS * N_DEV)
    index = lax.broadcasted_iota(jnp.int32, shape, item_axis)
    device = index % N_DEV
    order = (index // N_DEV) * (L // ITEMS) + device // 2
    part = device % 2
    longitude = lax.broadcasted_iota(
        jnp.int32, (1, NLON) if item_axis == 0 else (NLON, 1), 1 - item_axis
    )
    phase = longitude.astype(jnp.float32) * order.astype(jnp.float32) + 360.0 * part.astype(
        jnp.float32
    )
    phase = phase - 1440.0 * jnp.round(phase * (1.0 / 1440.0))
    angle = (360.0 - jnp.abs(phase)) * (math.pi / 720.0)
    square = angle * angle
    total = -1.0 / 39916800.0
    for term in (1.0 / 362880.0, -1.0 / 5040.0, 1.0 / 120.0, -1.0 / 6.0, 1.0):
        total = total * square + term
    return (total * angle).astype(jnp.bfloat16)


def exchange(values, axes, count):
    pairs = values.reshape(count, values.shape[0] // (2 * count), 2, 128)
    pairs = lax.all_to_all(pairs, axes, split_axis=0, concat_axis=0, tiled=True)
    return pairs.reshape(values.shape)


def regroup(values):
    return lax.all_to_all(values, "lon", split_axis=0, concat_axis=0, tiled=True)


def shards(cube_cells, block_source, block_weight, lift_in, lift_out, spectral):
    lat_index = lax.axis_index("lat")
    lon_index = lax.axis_index("lon")
    chip = lat_index * (N_LON // 2) + lon_index // 2
    odd = lon_index % 2
    far = SRC_DEV - RIM
    across = lax.ppermute(
        lax.dynamic_slice_in_dim(cube_cells, odd * far, RIM, 0),
        "lon",
        [(i, (i + 1) % N_LON if i % 2 else (i - 1) % N_LON) for i in range(N_LON)],
    )
    beside = lax.ppermute(
        lax.dynamic_slice_in_dim(cube_cells, (1 - odd) * far, RIM, 0),
        "lon",
        [(i, i ^ 1) for i in range(N_LON)],
    )
    offsets = (block_source[:, 0, :] - lon_index * SRC_DEV + RIM) % (N_LON * SRC_DEV)
    places = jnp.concatenate(
        [offsets.reshape(LAT_DEV * K), (odd * (RIM + SRC_DEV)).reshape(1).astype(jnp.int32)]
    )
    forward = fourier(0)
    matrices = jnp.concatenate([lift_out, lift_in], axis=0)
    inverse = fourier(1)
    weighted, plain = legendre(chip)
    columns = remap(places, across, cube_cells, beside, block_weight)
    columns = exchange(columns, "lon", N_LON)
    spectra = lift(columns, matrices, forward, (inverse, weighted, plain))
    spectra = exchange(spectra, ("lat", "lon"), N_DEV)
    analysis = regroup(analyse(spectra, weighted))
    mixed = regroup(mix(analysis, spectral))
    synthesis = exchange(synthesise(mixed, plain), ("lat", "lon"), N_DEV)
    field = exchange(invert(synthesis, inverse), "lon", N_LON)
    return unpack(field)


def solution(mesh):
    in_specs = (
        P(("lat", "lon"), None, None),
        P("lat", "lon", None),
        P("lat", "lon", None, None, None),
        P(),
        P(),
        P("lon", None, None),
    )
    out_specs = P("lat", "lon", None)
    return jax.shard_map(shards, mesh=mesh, in_specs=in_specs, out_specs=out_specs, check_vma=False)
```

```python
import math

import jax
import jax.numpy as jnp
from jax import lax
from jax.experimental import pallas as pl
from jax.experimental.pallas import tpu as pltpu
from jax.sharding import PartitionSpec as P

NLAT = 720
NLON = 1440
L = 384
CIN = 80
C = 256
TILE = 128
K = 4
SRC_DEV = 48
RIM = 24
LAT_DEV = 45
LON_DEV = 90
N_LAT = 16
N_LON = 16
N_DEV = N_LAT * N_LON

ROWS = 3
GROUPS = LAT_DEV // ROWS
ITEMS = 3
PIECES = 2 * ITEMS * ROWS
DEG = L // N_LON
LIFT_PAD = 2304
LATS = ROWS * N_DEV
MIB = 1024 * 1024


def params(mib):
    return pltpu.CompilerParams(vmem_limit_bytes=mib * MIB)


def whole():
    return pl.BlockSpec(memory_space=pltpu.VMEM)


def dot(a, b, dims=((1,), (0,))):
    return lax.dot_general(a, b, (dims, ((), ())), preferred_element_type=jnp.float32)


REMAP_STEPS = 2
STEP_GROUPS = N_LON // REMAP_STEPS
GROUP_ROWS = 2 * LON_DEV


def remap_kernel(offsets, across, own, beside, weight, out, tiles, packed):
    step = pl.program_id(0)

    @pl.when(step == 0)
    def _():
        place = offsets[LAT_DEV * K]
        tiles[pl.ds(place, RIM)] = across[...]
        tiles[pl.ds(RIM + SRC_DEV - place, RIM)] = beside[...]
        tiles[RIM : RIM + SRC_DEV] = own[...]

    def store(sub, values):
        for half in range(2):
            packed[pl.ds(sub * GROUP_ROWS + half, LON_DEV, stride=2), :] = values[
                :, half * 128 : (half + 1) * 128
            ]

    def fill(sub):
        columns = []
        for row in range(ROWS):
            base = ((step * STEP_GROUPS + sub) * ROWS + row) * K
            cells = jnp.concatenate([tiles[offsets[base + k]] for k in range(K)], axis=1)
            blocks = jnp.concatenate([weight[sub * ROWS + row, 0, k] for k in range(K)], axis=1)
            columns.append(dot(blocks, cells, ((1,), (1,))))
        columns.append(jnp.zeros((LON_DEV, C - ROWS * CIN), jnp.float32))
        store(sub, jnp.concatenate(columns, axis=1))

    for sub in range(STEP_GROUPS - 1):
        fill(sub)

    @pl.when(step < REMAP_STEPS - 1)
    def _():
        fill(STEP_GROUPS - 1)

    @pl.when(step == REMAP_STEPS - 1)
    def _():
        store(STEP_GROUPS - 1, jnp.zeros((LON_DEV, C), jnp.float32))

    out[...] = packed[...].astype(jnp.bfloat16)


def remap(offsets, across, own, beside, weight):
    return pl.pallas_call(
        remap_kernel,
        out_shape=jax.ShapeDtypeStruct((N_LON * GROUP_ROWS, 128), jnp.bfloat16),
        grid_spec=pltpu.PrefetchScalarGridSpec(
            num_scalar_prefetch=1,
            grid=(REMAP_STEPS,),
            in_specs=[
                pl.BlockSpec((RIM, CIN, TILE), lambda g, o: (0, 0, 0)),
                pl.BlockSpec((SRC_DEV, CIN, TILE), lambda g, o: (0, 0, 0)),
                pl.BlockSpec((RIM, CIN, TILE), lambda g, o: (0, 0, 0)),
                pl.BlockSpec(
                    (STEP_GROUPS * ROWS, 1, K, LON_DEV, TILE), lambda g, o: (g, 0, 0, 0, 0)
                ),
            ],
            out_specs=pl.BlockSpec((STEP_GROUPS * GROUP_ROWS, 128), lambda g, o: (g, 0)),
            scratch_shapes=[
                pltpu.VMEM((RIM + SRC_DEV + RIM, CIN, TILE), jnp.bfloat16),
                pltpu.VMEM((STEP_GROUPS * GROUP_ROWS, 128), jnp.float32),
            ],
        ),
        compiler_params=params(40),
        name="remap",
    )(offsets, across, own, beside, weight)


def lift_kernel(source, weights, forward, *rest):
    out, cols, packed, scratch, lifted, first, matrices, table, sems = rest[-9:]
    small = pltpu.make_async_copy(weights.at[: C + CIN], matrices, sems.at[2])
    small.start()
    fetch = pltpu.make_async_copy(source, cols, sems.at[0])
    fetch.start()
    copy = pltpu.make_async_copy(forward, table, sems.at[1])
    copy.start()
    first[...] = jnp.zeros_like(first)
    small.wait()
    for row in range(ROWS):
        first[row, row * CIN : (row + 1) * CIN] = matrices[C:]
    fetch.wait()
    packed[...] = cols[...].astype(jnp.float32)
    halves = [packed[pl.ds(h, NLON, stride=2), :] for h in range(2)]
    values = jnp.concatenate(halves, axis=1).astype(jnp.bfloat16)
    for row in range(ROWS):
        hidden = jax.nn.gelu(dot(values, first[row])).astype(jnp.bfloat16)
        lifted[:, row * C : (row + 1) * C] = dot(hidden, matrices[:C]).astype(jnp.bfloat16)
    copy.wait()
    for item in range(ITEMS):
        spectra = dot(table[item * N_DEV : (item + 1) * N_DEV], lifted[...])
        for piece in range(2 * ROWS):
            scratch[pl.ds(item * 2 * ROWS + piece, N_DEV, stride=PIECES), :] = spectra[
                :, piece * 128 : (piece + 1) * 128
            ]
    out[...] = scratch[...].astype(jnp.bfloat16)


def lift(cols, matrices, forward, tables):
    return pl.pallas_call(
        lift_kernel,
        out_shape=jax.ShapeDtypeStruct((N_DEV * PIECES, 128), jnp.bfloat16),
        in_specs=[pl.BlockSpec(memory_space=pl.ANY)] * (3 + len(tables)),
        out_specs=whole(),
        scratch_shapes=[
            pltpu.VMEM((2 * NLON, 128), jnp.bfloat16),
            pltpu.VMEM((2 * NLON, 128), jnp.float32),
            pltpu.VMEM((N_DEV * PIECES, 128), jnp.float32),
            pltpu.VMEM((NLON, ROWS * C), jnp.bfloat16),
            pltpu.VMEM((ROWS, C, C), jnp.bfloat16),
            pltpu.VMEM((C + CIN, C), jnp.bfloat16),
            pltpu.VMEM((ITEMS * N_DEV, NLON), jnp.bfloat16),
            pltpu.SemaphoreType.DMA((3,)),
        ],
        compiler_params=params(48),
        name="lift",
    )(cols, matrices, forward, *tables)


def legendre_kernel(rise, fall, start, initial, restore, factor, cosine, quad, weighted, plain, table):
    tiles = LATS // 128
    cos = [cosine[:, t * 128 : (t + 1) * 128] for t in range(tiles)]
    init = [initial[:, t * 128 : (t + 1) * 128] for t in range(tiles)]

    def advance(block, carry):
        current, earlier = carry
        for step in range(8):
            degree = block * 8 + step
            up, down, on = rise[degree], fall[degree], start[degree]
            latest = []
            for t in range(tiles):
                value = up * (cos[t] * current[t] - down * earlier[t]) + on * init[t]
                table[t, pl.ds(pl.multiple_of(degree * 8, 8), 8), :] = value
                latest.append(value)
            current, earlier = tuple(latest), current
        return current, earlier

    zero = tuple(jnp.zeros((8, 128), jnp.float32) for _ in range(tiles))
    lax.fori_loop(0, L // 8, advance, (zero, zero))
    for item in range(ITEMS):
        for t in range(tiles):
            lanes = slice(t * 128, (t + 1) * 128)
            values = table[t, pl.ds(item, L, stride=8), :] * restore[item : item + 1, lanes]
            weighted[item, :, lanes] = (values * quad[0:1, lanes]).astype(jnp.bfloat16)
            values = values * factor[item : item + 1, lanes]
            plain[item, lanes, :] = values.T.astype(jnp.bfloat16)


def legendre(chip):
    lane = jnp.arange(LATS, dtype=jnp.int32)
    row, device = lane // N_DEV, lane % N_DEV
    band, group = device // N_LON, device % N_LON
    held = (group < GROUPS)[None, :]
    latitude = band * LAT_DEV + jnp.minimum(group, GROUPS - 1) * ROWS + row
    colatitude = (latitude.astype(jnp.float32) + 0.5) * (math.pi / NLAT)
    cosine = jnp.cos(colatitude)[None, :]
    sine = jnp.sin(colatitude)[None, :]
    slot = jnp.arange(8, dtype=jnp.int32)
    order = (jnp.minimum(slot, ITEMS - 1) * (L // ITEMS) + chip).astype(jnp.float32)
    order_col = order[:, None]
    log_scale = (
        0.5
        * (
            jnp.log(2.0 * order_col + 1.0)
            - math.log(4.0 * math.pi)
            + lax.lgamma(2.0 * order_col + 1.0)
            - 2.0 * lax.lgamma(order_col + 1.0)
            - order_col * math.log(4.0)
        )
        + order_col * jnp.log(sine)
    )
    initial = jnp.exp(jnp.minimum(log_scale + 80.0, 0.0))
    restore = jnp.where(held, jnp.exp(jnp.maximum(log_scale, -80.0)), 0.0)
    quad = jnp.broadcast_to(sine * (math.pi / NLAT) * (2.0 * math.pi / NLON), (8, LATS))
    factor = jnp.broadcast_to(jnp.where(order_col == 0.0, 1.0, 2.0), (8, LATS))
    degree = jnp.arange(L, dtype=jnp.int32).astype(jnp.float32)[:, None, None]
    order_row = order[None, :, None]
    square = degree * degree
    rising = jnp.sqrt(
        jnp.maximum(4.0 * square - 1.0, 1.0) / jnp.maximum(square - order_row * order_row, 1.0)
    )
    shifted = (degree - 1.0) * (degree - 1.0)
    falling = jnp.sqrt(
        jnp.maximum(shifted - order_row * order_row, 0.0) / jnp.maximum(4.0 * shifted - 1.0, 1.0)
    )
    start = jnp.where(degree == order_row, 1.0, 0.0)
    spread = lambda values: jnp.broadcast_to(values, (L, 8, 128))
    return pl.pallas_call(
        legendre_kernel,
        out_shape=(
            jax.ShapeDtypeStruct((ITEMS, L, LATS), jnp.bfloat16),
            jax.ShapeDtypeStruct((ITEMS, LATS, L), jnp.bfloat16),
        ),
        in_specs=[whole()] * 8,
        out_specs=(whole(), whole()),
        scratch_shapes=[pltpu.VMEM((LATS // 128, L * 8, 128), jnp.float32)],
        compiler_params=params(40),
        name="legendre",
    )(
        spread(rising),
        spread(falling),
        spread(start),
        initial,
        restore,
        factor,
        jnp.broadcast_to(cosine, (8, LATS)),
        quad,
    )


def analyse_kernel(pieces, weighted, out, scratch):
    scratch[...] = pieces[...].astype(jnp.float32)
    for item in range(ITEMS):
        rows = []
        for row in range(ROWS):
            place = (item * ROWS + row) * 2
            halves = [scratch[pl.ds(place + h, N_DEV, stride=PIECES), :] for h in range(2)]
            rows.append(jnp.concatenate(halves, axis=1).astype(jnp.bfloat16))
        spectra = jnp.concatenate(rows, axis=0)
        result = dot(weighted[item], spectra).reshape(N_LON, DEG, C)
        out[:, item * DEG : (item + 1) * DEG, :] = result.astype(jnp.bfloat16)


def analyse(pieces, weighted):
    return pl.pallas_call(
        analyse_kernel,
        out_shape=jax.ShapeDtypeStruct((N_LON, ITEMS * DEG, C), jnp.bfloat16),
        in_specs=[whole()] * 2,
        out_specs=whole(),
        scratch_shapes=[pltpu.VMEM((N_DEV * PIECES, 128), jnp.float32)],
        compiler_params=params(40),
        name="analyse",
    )(pieces, weighted)


def mix_kernel(pieces, spectral, out, source, result):
    count = N_LON * ITEMS
    values = pieces[...].astype(jnp.float32).reshape(count * DEG, C)
    source[0] = values[:, :128]
    source[1] = values[:, 128:]
    for degree in range(DEG):
        halves = [source[h, pl.ds(degree, count, stride=DEG), :] for h in range(2)]
        values = jnp.concatenate(halves, axis=1).astype(jnp.bfloat16)
        mixed = dot(values, spectral[degree])
        for h in range(2):
            result[h, pl.ds(degree, count, stride=DEG), :] = mixed[:, h * 128 : (h + 1) * 128]
    for h in range(2):
        values = result[h].reshape(N_LON, ITEMS * DEG, 128)
        out[:, :, h * 128 : (h + 1) * 128] = values.astype(jnp.bfloat16)


def mix(pieces, spectral):
    return pl.pallas_call(
        mix_kernel,
        out_shape=jax.ShapeDtypeStruct((N_LON, ITEMS * DEG, C), jnp.bfloat16),
        in_specs=[whole()] * 2,
        out_specs=whole(),
        scratch_shapes=[pltpu.VMEM((2, N_LON * ITEMS * DEG, 128), jnp.float32)] * 2,
        compiler_params=params(40),
        name="mix",
    )(pieces, spectral)


def synthesise_kernel(pieces, plain, out, scratch):
    for item in range(ITEMS):
        values = pieces[...].astype(jnp.float32)[:, item * DEG : (item + 1) * DEG, :]
        mixed = values.reshape(L, C).astype(jnp.bfloat16)
        result = dot(plain[item], mixed)
        for row in range(ROWS):
            for half in range(2):
                place = (item * ROWS + row) * 2 + half
                scratch[pl.ds(place, N_DEV, stride=PIECES), :] = result[
                    row * N_DEV : (row + 1) * N_DEV, half * 128 : (half + 1) * 128
                ]
    out[...] = scratch[...].astype(jnp.bfloat16)


def synthesise(pieces, plain):
    return pl.pallas_call(
        synthesise_kernel,
        out_shape=jax.ShapeDtypeStruct((N_DEV * PIECES, 128), jnp.bfloat16),
        in_specs=[whole()] * 2,
        out_specs=whole(),
        scratch_shapes=[pltpu.VMEM((N_DEV * PIECES, 128), jnp.float32)],
        compiler_params=params(40),
        name="synthesise",
    )(pieces, plain)


TILES = 2 * ROWS
INVERT_BLOCK = NLON // 3


def inverse_kernel(pieces, inverse, out, scratch, packed):
    scratch[...] = pieces[...].astype(jnp.float32)
    items = []
    for item in range(ITEMS):
        places = [item * TILES + piece for piece in range(TILES)]
        parts = [scratch[pl.ds(place, N_DEV, stride=PIECES), :] for place in places]
        items.append(jnp.concatenate(parts, axis=1).astype(jnp.bfloat16))
    spectra = jnp.concatenate(items, axis=0)
    for start in range(0, NLON, INVERT_BLOCK):
        field = dot(inverse[start : start + INVERT_BLOCK], spectra)
        for piece in range(TILES):
            packed[pl.ds(start * TILES + piece, INVERT_BLOCK, stride=TILES), :] = field[
                :, piece * 128 : (piece + 1) * 128
            ]
    out[...] = packed[...].astype(jnp.bfloat16)


def invert(pieces, inverse):
    return pl.pallas_call(
        inverse_kernel,
        out_shape=jax.ShapeDtypeStruct((NLON * TILES, 128), jnp.bfloat16),
        in_specs=[whole()] * 2,
        out_specs=whole(),
        scratch_shapes=[
            pltpu.VMEM((N_DEV * PIECES, 128), jnp.float32),
            pltpu.VMEM((NLON * TILES, 128), jnp.float32),
        ],
        compiler_params=params(48),
        name="invert",
    )(pieces, inverse)


UNPACK_PARTS = 5


def unpack_kernel(pieces, out, packed, rows, sems):
    count = GROUPS // UNPACK_PARTS
    size = count * LON_DEV * TILES
    copies = []
    for part in range(UNPACK_PARTS):
        packed[...] = pieces[part * size : (part + 1) * size].astype(jnp.float32)
        for row in range(count * ROWS):
            place = row // ROWS * LON_DEV * TILES + row % ROWS * 2
            halves = [packed[pl.ds(place + h, LON_DEV, stride=TILES), :] for h in range(2)]
            rows[part, row] = jnp.concatenate(halves, axis=1).astype(jnp.bfloat16)
        block = pl.ds(part * count * ROWS, count * ROWS)
        copies.append(pltpu.make_async_copy(rows.at[part], out.at[block], sems.at[part]))
        copies[-1].start()
    for copy in copies:
        copy.wait()


def unpack(pieces):
    count = GROUPS // UNPACK_PARTS
    return pl.pallas_call(
        unpack_kernel,
        out_shape=jax.ShapeDtypeStruct((LAT_DEV, LON_DEV, C), jnp.bfloat16),
        in_specs=[whole()],
        out_specs=pl.BlockSpec(memory_space=pl.ANY),
        scratch_shapes=[
            pltpu.VMEM((count * LON_DEV * TILES, 128), jnp.float32),
            pltpu.VMEM((UNPACK_PARTS, count * ROWS, LON_DEV, C), jnp.bfloat16),
            pltpu.SemaphoreType.DMA((UNPACK_PARTS,)),
        ],
        compiler_params=params(32),
        name="unpack",
    )(pieces)


def fourier(item_axis):
    shape = (ITEMS * N_DEV, 1) if item_axis == 0 else (1, ITEMS * N_DEV)
    index = lax.broadcasted_iota(jnp.int32, shape, item_axis)
    device = index % N_DEV
    order = (index // N_DEV) * (L // ITEMS) + device // 2
    part = device % 2
    longitude = lax.broadcasted_iota(
        jnp.int32, (1, NLON) if item_axis == 0 else (NLON, 1), 1 - item_axis
    )
    phase = longitude.astype(jnp.float32) * order.astype(jnp.float32) + 360.0 * part.astype(
        jnp.float32
    )
    phase = phase - 1440.0 * jnp.round(phase * (1.0 / 1440.0))
    angle = (360.0 - jnp.abs(phase)) * (math.pi / 720.0)
    square = angle * angle
    total = -1.0 / 39916800.0
    for term in (1.0 / 362880.0, -1.0 / 5040.0, 1.0 / 120.0, -1.0 / 6.0, 1.0):
        total = total * square + term
    return (total * angle).astype(jnp.bfloat16)


def exchange(values, axes, count):
    pairs = values.reshape(count, values.shape[0] // (2 * count), 2, 128)
    pairs = lax.all_to_all(pairs, axes, split_axis=0, concat_axis=0, tiled=True)
    return pairs.reshape(values.shape)


def regroup(values):
    return lax.all_to_all(values, "lon", split_axis=0, concat_axis=0, tiled=True)


def shards(cube_cells, block_source, block_weight, lift_in, lift_out, spectral):
    lat_index = lax.axis_index("lat")
    lon_index = lax.axis_index("lon")
    chip = lat_index * (N_LON // 2) + lon_index // 2
    odd = lon_index % 2
    far = SRC_DEV - RIM
    across = lax.ppermute(
        lax.dynamic_slice_in_dim(cube_cells, odd * far, RIM, 0),
        "lon",
        [(i, (i + 1) % N_LON if i % 2 else (i - 1) % N_LON) for i in range(N_LON)],
    )
    beside = lax.ppermute(
        lax.dynamic_slice_in_dim(cube_cells, (1 - odd) * far, RIM, 0),
        "lon",
        [(i, i ^ 1) for i in range(N_LON)],
    )
    offsets = (block_source[:, 0, :] - lon_index * SRC_DEV + RIM) % (N_LON * SRC_DEV)
    places = jnp.concatenate(
        [offsets.reshape(LAT_DEV * K), (odd * (RIM + SRC_DEV)).reshape(1).astype(jnp.int32)]
    )
    forward = fourier(0)
    matrices = jnp.pad(jnp.concatenate([lift_out, lift_in], axis=0), ((0, LIFT_PAD), (0, 0)))
    inverse = fourier(1)
    weighted, plain = legendre(chip)
    columns = remap(places, across, cube_cells, beside, block_weight)
    columns = exchange(columns, "lon", N_LON)
    spectra = lift(columns, matrices, forward, (inverse, weighted, plain))
    spectra = exchange(spectra, ("lat", "lon"), N_DEV)
    analysis = regroup(analyse(spectra, weighted))
    mixed = regroup(mix(analysis, spectral))
    synthesis = exchange(synthesise(mixed, plain), ("lat", "lon"), N_DEV)
    field = exchange(invert(synthesis, inverse), "lon", N_LON)
    return unpack(field)


def solution(mesh):
    in_specs = (
        P(("lat", "lon"), None, None),
        P("lat", "lon", None),
        P("lat", "lon", None, None, None),
        P(),
        P(),
        P("lon", None, None),
    )
    out_specs = P("lat", "lon", None)
    return jax.shard_map(shards, mesh=mesh, in_specs=in_specs, out_specs=out_specs, check_vma=False)
```
